32 devices in a mesh: ep: 16 (over z, y, core), rep: 2 (over x).
Axes of the slice: x: 2, y: 2, z: 4, core: 2. Of those that a mesh axis runs over, the one named last changes fastest.
Arguments:
- residual: bfloat16 [512, 2048], P('ep'), may hold values from -6 to 6
- query_latent: bfloat16 [512, 8192], P(('ep', 'rep')), may hold values from -32.5 to 32.5
- query_rope: bfloat16 [512, 1024], P(('ep', 'rep')), may hold values from -4 to 4
- cache_latent: bfloat16 [1024, 32, 512], P(('ep', 'rep')), may hold values from -4.6 to 4.6
- cache_rope: bfloat16 [1024, 2048], P(('ep', 'rep')), may hold values from -4 to 4
- page_table: int32 [512, 9], P(('ep', 'rep')), may hold values from 0 to 31, as said below
- lengths: int32 [512], P(('ep', 'rep')), may hold values from 257 to 288, as said below
- value_up: bfloat16 [16, 512, 128], P('rep'), may hold values from -0.25 to 0.25
- out_proj: bfloat16 [2048, 2048], P('rep'), may hold values from -0.125 to 0.125
- routes: int32 [512, 6], P('ep'), may hold values from 0 to 15, all different within a row; in each aligned block of 32 rows (0 to 31, 32 to 63, ...) at most 24 rows name the same one
- route_weight: float32 [512, 6], P('ep'), may hold values from 0.05 to 0.6
- placement: int32 [16], replicated, may hold values from 0 to 15, each once
- expert_gate: bfloat16 [16, 2048, 1408], P('ep', None, 'rep'), may hold values from -0.125 to 0.125
- expert_up: bfloat16 [16, 2048, 1408], P('ep', None, 'rep'), may hold values from -0.125 to 0.125
- expert_down: bfloat16 [16, 1408, 2048], P('ep', 'rep'), may hold values from -0.15625 to 0.15625
- shared_gate: bfloat16 [2048, 1408], P(None, 'rep'), may hold values from -0.125 to 0.125
- shared_up: bfloat16 [2048, 1408], P(None, 'rep'), may hold values from -0.125 to 0.125
- shared_down: bfloat16 [1408, 2048], P('rep'), may hold values from -0.15625 to 0.15625
- norm_gain: float32 [2048], replicated, may hold values from 0.5 to 1.5
Outputs:
- normed: bfloat16 [512, 2048], P(('ep', 'rep'))
The draws below stay inside these ranges and needn't reach their ends.
Inputs may be any that keep to these rules, and one draw needn't show every extreme that they name: `page_table`: entries number the 32 pages of the row's own device. A device's rows come in consecutive groups of 8 that share their first 8 entries; all other entries of a device are distinct. `lengths`: every row's context covers its shared prompt; the last row of every device has the greatest length. `routes`: within the 32 rows of one index of ep, no expert is named by more than 24 rows, a bound that some block reaches. `placement`: each slot holds exactly one expert.
All inputs are finite; a program needn't handle non-finite values.
Results may differ from the reference program's by a relative error of at most 0.014.
Values may be sent and summed in bfloat16 or wider, within the bound.
No kernel may reach another device: no remote copies, remote signals or barrier semaphores. Data moves between devices by JAX's collectives and lax.ppermute only.
A program may use at most 128 MiB of HBM per device.

```python
import math
import jax
import jax.numpy as jnp
import numpy as np
from jax import lax

D = 2048
HEADS = 16
LATENT = 512
ROPE = 64
VHEAD = 128
FF = 1408
TOP = 6
ROWS_DEV = 16
SHARE = 8
PAGE = 32
PREFIX = 8
PRIVATE = 1
PAGES_SEQ = 9
POOL = 32
PAGES_ALL = 1024
EXPERTS = 16
GROUP_ROWS = 32
TOKENS = 512
CAP = 24
N_EP = 16
N_REP = 2


def page_layout(key):
    device_count = TOKENS // ROWS_DEV
    page_keys = jax.random.split(jax.random.fold_in(key, 11), device_count)
    shuffles = jax.vmap(lambda one_key: jax.random.permutation(one_key, POOL))(page_keys).astype(jnp.int32)
    row_ids = jnp.arange(ROWS_DEV, dtype=jnp.int32)
    col_ids = jnp.arange(PAGES_SEQ, dtype=jnp.int32)
    group_total = ROWS_DEV // SHARE
    prefix_pick = (row_ids // SHARE)[:, None] * PREFIX + col_ids[None, :]
    private_pick = group_total * PREFIX + row_ids[:, None] * PRIVATE + (col_ids[None, :] - PREFIX)
    picks = jnp.where(col_ids[None, :] < PREFIX, prefix_pick, private_pick)
    return shuffles[:, picks].reshape(TOKENS, PAGES_SEQ).astype(jnp.int32)


def first_slots(key):
    drawn = jax.random.normal(jax.random.fold_in(key, 16), (PAGES_ALL, LATENT), jnp.float32)
    return jnp.clip(drawn, -4.0, 4.0)


def draw_page_table(key, part):
    return page_layout(key)


def draw_lengths(key, part):
    low_end = PREFIX * PAGE + 1
    high_end = PAGES_SEQ * PAGE
    drawn = jax.random.randint(jax.random.fold_in(key, 12), (TOKENS,), low_end, high_end + 1, dtype=jnp.int32)
    return drawn.at[ROWS_DEV - 1::ROWS_DEV].set(high_end)


def draw_cache_latent(key, part):
    drawn = jax.random.normal(jax.random.fold_in(key, 13), (PAGES_ALL, PAGE, LATENT), jnp.float32)
    pages = jnp.clip(drawn, -4.0, 4.0)
    leading = first_slots(key)
    pages = pages.at[:, 0, :].set(leading)
    return pages.astype(jnp.bfloat16)


def draw_query_latent(key, part):
    drawn = jax.random.normal(jax.random.fold_in(key, 15), (TOKENS, HEADS, LATENT), jnp.float32)
    drawn = 0.6 * jnp.clip(drawn, -4.0, 4.0)
    return drawn.reshape(TOKENS, HEADS * LATENT).astype(jnp.bfloat16)


def steps_of(own_key, extent, cuts, least, high):
    def one(dim, blocks):
        heights = jax.random.uniform(jax.random.fold_in(jax.random.fold_in(own_key, 6), dim), (blocks,), jnp.float32, least / len(cuts), high / len(cuts))
        return jnp.repeat(jnp.exp(heights), extent[dim] // blocks).reshape((-1,) + (1,) * (len(extent) - dim - 1))

    level = one(*cuts[0])
    for cut in cuts[1:]:
        level = level * one(*cut)
    return level


def deal_out(key, own, number, rows, amount, top, bound, lean):
    sequence = jax.random.permutation(key, amount)
    packed, usual = portions_of(amount, rows * top, bound, lean, True), portions_of(amount, rows * top, bound, lean, False)
    places = jnp.arange(amount)

    def named(sizes, rotation):
        used = int((sizes > 0).sum())
        fixed = max(1, used // 4)
        moved = fixed + (places - fixed + rotation * (used - fixed)) % max(1, amount - fixed)
        return jnp.zeros((amount,), jnp.int32).at[sequence[jnp.where(places < fixed, places, moved)]].set(jnp.asarray(sizes, jnp.int32))

    sizes = jnp.where(number % 4 == 0, named(packed, number // 4), named(usual, number - number // 4 - 1))
    mixed = jax.random.permutation(jax.random.fold_in(own, 3), amount)
    source_of, receiver = mixed[0:amount // 2 * 2:2], mixed[1:amount // 2 * 2:2]
    margin = jnp.minimum(sizes[source_of] - 1, bound - sizes[receiver]) // 2
    margin = jnp.where((source_of == sequence[0]) | (receiver == sequence[0]) | (sizes[receiver] == 0), 0, jnp.maximum(margin, 0))
    moved = jax.random.randint(jax.random.fold_in(own, 4), (amount // 2,), 0, 1 << 20) % (margin + 1)
    sizes = sizes.at[source_of].add(-moved).at[receiver].add(moved)
    members = jnp.searchsorted(jnp.cumsum(sizes), jnp.arange(rows * top), side="right").astype(jnp.int32)
    grid = members.reshape(top, rows).T
    grid = grid[jax.random.permutation(jax.random.fold_in(own, 1), rows)]
    rotation = jax.random.randint(jax.random.fold_in(own, 2), (rows, 1), 0, top)
    return jnp.take_along_axis(grid, (jnp.arange(top)[None, :] + rotation) % top, axis=1)


def portions_of(count, total, limit, skew, full):
    portions = [(1 << 20) // math.isqrt(standing ** skew) + 1 for standing in range(1, count + 1)]
    largest = limit if full else min(limit, max(-(-total // count), total * portions[0] // sum(portions)))
    least = 1 if total - largest >= count - 1 else 0
    given, surplus = [largest] + [least] * (count - 1), total - largest - least * (count - 1)
    while surplus > 0:
        movable = [i for i in range(1, count) if given[i] < largest] or [i for i in range(1, count) if given[i] < limit]
        pool, remaining = sum([portions[i] for i in movable]), surplus
        for i in movable:
            addition = min(limit - given[i], max(1, remaining * portions[i] // pool), surplus)
            given[i] = given[i] + addition
            surplus = surplus - addition
    return np.array(given)


def normal_values(own_key, shape, deviation, reach, cuts=(), kind=jnp.bfloat16):
    result = jax.random.normal(own_key, shape, jnp.float32) * deviation
    if len(cuts) > 0:
        result = steps_of(own_key, shape, cuts, -0.22, 0.18) * result
    return jnp.clip(result, min=-reach, max=reach).astype(kind)


def setup_inputs(seed: int = 0) -> dict:
    streams_of = jax.random.split(jax.random.key(seed), 20)
    residual = normal_values(streams_of[0], (TOKENS, D), 1.0, 6.0, ((0, 16),))
    query_latent = draw_query_latent(jax.random.fold_in(streams_of[19], 71), 0)
    query_rope = normal_values(streams_of[2], (TOKENS, HEADS * ROPE), 1.0, 4.0, ((0, 32),))
    cache_latent = draw_cache_latent(jax.random.fold_in(streams_of[19], 71), 0)
    cache_rope = normal_values(streams_of[4], (PAGES_ALL, PAGE * ROPE), 1.0, 4.0, ((0, 32),))
    page_table = draw_page_table(jax.random.fold_in(streams_of[19], 71), 0)
    lengths = draw_lengths(jax.random.fold_in(streams_of[19], 71), 0)
    value_up = normal_values(streams_of[7], (HEADS, LATENT, VHEAD), LATENT ** -0.5, 0.25, ((0, 2),))
    out_proj = normal_values(streams_of[8], (HEADS * VHEAD, D), (HEADS * VHEAD) ** -0.5, 0.125, ((0, 2),))
    routes_keys = jax.random.split(jax.random.fold_in(streams_of[9], 1), TOKENS // GROUP_ROWS)
    routes_turns = jax.random.permutation(jax.random.fold_in(streams_of[9], 3), TOKENS // GROUP_ROWS)
    routes = jax.vmap(lambda own, number: deal_out(jax.random.fold_in(streams_of[9], 2), own, number, GROUP_ROWS, EXPERTS, TOP, CAP, 2))(routes_keys, routes_turns).reshape((TOKENS, TOP))
    route_weight = jnp.clip(0.05 + 0.55 * jax.random.uniform(streams_of[10], (TOKENS, TOP), jnp.float32) ** steps_of(streams_of[10], (TOKENS, TOP), ((0, 16),), -0.2, 0.2), 0.05, 0.6)
    placement = jax.random.permutation(streams_of[11], EXPERTS).astype(jnp.int32)
    expert_gate = normal_values(streams_of[12], (EXPERTS, D, FF), D ** -0.5, 0.125, ((0, 16), (2, 2)))
    expert_up = normal_values(streams_of[13], (EXPERTS, D, FF), D ** -0.5, 0.125, ((0, 16), (2, 2)))
    expert_down = normal_values(streams_of[14], (EXPERTS, FF, D), FF ** -0.5, 0.15625, ((0, 16), (1, 2)))
    shared_gate = normal_values(streams_of[15], (D, FF), D ** -0.5, 0.125, ((1, 2),))
    shared_up = normal_values(streams_of[16], (D, FF), D ** -0.5, 0.125, ((1, 2),))
    shared_down = normal_values(streams_of[17], (FF, D), FF ** -0.5, 0.15625, ((0, 2),))
    norm_gain = jnp.clip(1.0 + 0.1 * jax.random.normal(streams_of[18], (D,), jnp.float32), 0.5, 1.5)
    return dict(residual=residual, query_latent=query_latent, query_rope=query_rope, cache_latent=cache_latent, cache_rope=cache_rope, page_table=page_table, lengths=lengths, value_up=value_up, out_proj=out_proj, routes=routes, route_weight=route_weight, placement=placement, expert_gate=expert_gate, expert_up=expert_up, expert_down=expert_down, shared_gate=shared_gate, shared_up=shared_up, shared_down=shared_down, norm_gain=norm_gain)


EPSILON = 1e-06

def attend_block(query_latent, query_rope, keys_lat, keys_rope, lengths):
    row_count = keys_lat.shape[0]
    key_span = keys_lat.shape[1]
    query_lat = query_latent.reshape(row_count, HEADS, LATENT).astype(jnp.float32)
    query_rot = query_rope.reshape(row_count, HEADS, ROPE).astype(jnp.float32)
    score_scale = 1.0 / math.sqrt(VHEAD + ROPE)
    scores = (jnp.einsum('thr,tlr->thl', query_lat, keys_lat.astype(jnp.float32)) + jnp.einsum('thr,tlr->thl', query_rot, keys_rope.astype(jnp.float32))) * score_scale
    live_mask = (jnp.arange(key_span, dtype=jnp.int32)[None, :] < lengths[:, None])[:, None, :]
    masked = jnp.where(live_mask, scores, -jnp.inf)
    row_peak = lax.optimization_barrier(jnp.max(masked, axis=2, keepdims=True))
    expons = jnp.where(live_mask, jnp.exp(scores - row_peak), 0.0)
    probs = (expons / lax.optimization_barrier(jnp.sum(expons, axis=2, keepdims=True))).astype(jnp.bfloat16)
    latent_out = jnp.einsum('thl,tlr->thr', probs.astype(jnp.float32), keys_lat.astype(jnp.float32))
    return latent_out.astype(jnp.bfloat16)

def reference(residual, query_latent, query_rope, cache_latent, cache_rope, page_table, lengths, value_up, out_proj, routes, route_weight, placement, expert_gate, expert_up, expert_down, shared_gate, shared_up, shared_down, norm_gain):
    block_count = TOKENS // ROWS_DEV
    key_span = PAGES_SEQ * PAGE

    def one_block(block_index):
        start_row = block_index * ROWS_DEV
        table = lax.dynamic_slice_in_dim(page_table, start_row, ROWS_DEV, 0) + block_index * POOL
        keys_lat = cache_latent[table].reshape(ROWS_DEV, key_span, LATENT)
        keys_rope = cache_rope[table].reshape(ROWS_DEV, key_span, ROPE)
        block_query = lax.dynamic_slice_in_dim(query_latent, start_row, ROWS_DEV, 0)
        block_rope = lax.dynamic_slice_in_dim(query_rope, start_row, ROWS_DEV, 0)
        block_len = lax.dynamic_slice_in_dim(lengths, start_row, ROWS_DEV, 0)
        return attend_block(block_query, block_rope, keys_lat, keys_rope, block_len)
    latent_out = lax.map(one_block, jnp.arange(block_count, dtype=jnp.int32)).reshape(TOKENS, HEADS, LATENT)
    head_out = jnp.einsum('thr,hrv->thv', latent_out.astype(jnp.float32), value_up.astype(jnp.float32)).astype(jnp.bfloat16)
    attended = jnp.dot(head_out.reshape(TOKENS, HEADS * VHEAD), out_proj, preferred_element_type=jnp.float32).astype(jnp.bfloat16)
    hidden = (residual.astype(jnp.float32) + attended.astype(jnp.float32)).astype(jnp.bfloat16)
    shared_act = (jax.nn.silu(jnp.dot(hidden, shared_gate, preferred_element_type=jnp.float32)) * jnp.dot(hidden, shared_up, preferred_element_type=jnp.float32)).astype(jnp.bfloat16)
    shared_out = jnp.dot(shared_act, shared_down, preferred_element_type=jnp.float32)
    flat_routes = routes.reshape(-1)
    flat_weight = route_weight.reshape(-1)
    limit_rows = min(TOKENS * TOP, N_EP * CAP)
    quarter_width = FF // N_REP

    def one_expert(total, expert):
        hits = flat_routes == expert
        chosen = jnp.nonzero(hits, size=limit_rows, fill_value=0)[0].astype(jnp.int32)
        hit_count = jnp.sum(hits.astype(jnp.int32))
        valid = jnp.arange(limit_rows, dtype=jnp.int32) < hit_count
        token_index = chosen // TOP
        picked_rows = hidden[token_index]
        slot_index = placement[expert]
        gate_values = jnp.dot(picked_rows, expert_gate[slot_index], preferred_element_type=jnp.float32)
        up_values = jnp.dot(picked_rows, expert_up[slot_index], preferred_element_type=jnp.float32)
        activated = (jax.nn.silu(gate_values) * up_values).astype(jnp.bfloat16)
        down_rows = expert_down[slot_index]
        expert_out = jnp.zeros((limit_rows, D), jnp.float32)
        for quarter in range(N_REP):
            part_out = jnp.dot(activated[:, quarter * quarter_width:(quarter + 1) * quarter_width], down_rows[quarter * quarter_width:(quarter + 1) * quarter_width], preferred_element_type=jnp.float32).astype(jnp.bfloat16)
            expert_out = expert_out + part_out.astype(jnp.float32)
        weight_used = jnp.where(valid, flat_weight[chosen], jnp.zeros((), flat_weight.dtype))
        return (total.at[token_index].add(expert_out * weight_used[:, None]), None)
    routed, _ = lax.scan(one_expert, jnp.zeros((TOKENS, D), jnp.float32), jnp.arange(EXPERTS, dtype=jnp.int32))
    mixed = hidden.astype(jnp.float32) + shared_out + routed
    inverse = lax.rsqrt(lax.optimization_barrier(jnp.mean(mixed * mixed, axis=1, keepdims=True)) + EPSILON)
    return (mixed * inverse * norm_gain).astype(jnp.bfloat16)
```

```python
import functools
import math

import jax
import jax.numpy as jnp
from jax import lax
from jax.experimental import pallas as pl
from jax.experimental.pallas import tpu as pltpu
from jax.sharding import PartitionSpec as P

ROPE = 64
VHEAD = 128
LANES = 128
EPSILON = 1e-06
AXES = ("ep", "rep")
MIB = 1024 * 1024
NT = (((1,), (1,)), ((), ()))


def attend_kernel(
    block_ref, table_ref, lengths_ref, query_ref, rot_ref, pages_ref, rope_ref, out_ref, keys_rope
):
    del block_ref
    rows, span = table_ref.shape
    pages, page_len, latent = pages_ref.shape
    keys = pages * page_len
    heads = out_ref.shape[0] // rows
    for pair in range(page_len // 2):
        both = rope_ref[:, pair * LANES : (pair + 1) * LANES].astype(jnp.float32)
        keys_rope[pl.ds(2 * pair, pages, stride=page_len), :] = both
        keys_rope[pl.ds(2 * pair + 1, pages, stride=page_len), :] = pltpu.roll(both, ROPE, 1)
    key_ids = lax.broadcasted_iota(jnp.int32, (rows, keys), 1)
    page_of, slot_of = key_ids // page_len, key_ids % page_len
    lengths = lengths_ref[...]
    count = jnp.zeros((rows, keys), jnp.float32)
    for step in range(span):
        live = (table_ref[:, step : step + 1] == page_of) & (slot_of + step * page_len < lengths)
        count = count + jnp.where(live, 1.0, 0.0)
    low = lax.broadcasted_iota(jnp.int32, (rows, LANES), 1) < ROPE
    lat_parts, rot_parts = [], []
    for head in range(heads):
        lat_parts.append(query_ref[:, head * latent : (head + 1) * latent])
        pair = rot_ref[:, head // 2 * LANES : (head // 2 + 1) * LANES].astype(jnp.float32)
        if head % 2:
            pair = pltpu.roll(pair, ROPE, 1)
        rot_parts.append(jnp.where(low, pair, 0.0).astype(jnp.bfloat16))
    query = jnp.concatenate(lat_parts, axis=0)
    rot = jnp.concatenate(rot_parts, axis=0)
    key_lat = pages_ref[...].reshape(keys, latent)
    key_rot = keys_rope[...].astype(jnp.bfloat16)
    scores = (
        lax.dot_general(query, key_lat, NT, preferred_element_type=jnp.float32)
        + lax.dot_general(rot, key_rot, NT, preferred_element_type=jnp.float32)
    ) * (1.0 / math.sqrt(VHEAD + ROPE))
    scores = scores.reshape(heads, rows, keys)
    masked = jnp.where(count[None] > 0.0, scores, -jnp.inf)
    peak = jnp.max(masked, axis=2, keepdims=True)
    expons = jnp.exp(masked - peak) * count[None]
    probs = (expons / jnp.sum(expons, axis=2, keepdims=True)).astype(jnp.bfloat16)
    out_ref[...] = jnp.dot(
        probs.reshape(heads * rows, keys), key_lat, preferred_element_type=jnp.float32
    ).astype(jnp.bfloat16)


def attend(block, heads, query_latent, query_rope, cache_latent, cache_rope, page_table, lengths):
    rows = page_table.shape[0]
    pages, page_len, latent = cache_latent.shape
    whole = lambda *shape: pl.BlockSpec(shape, lambda i, s: (0,) * len(shape))
    return pl.pallas_call(
        attend_kernel,
        grid_spec=pltpu.PrefetchScalarGridSpec(
            num_scalar_prefetch=1,
            grid=(1,),
            in_specs=[
                whole(*page_table.shape),
                whole(rows, 1),
                pl.BlockSpec((rows, heads * latent), lambda i, s: (0, s[0])),
                pl.BlockSpec((rows, heads * ROPE), lambda i, s: (0, s[0])),
                whole(*cache_latent.shape),
                whole(*cache_rope.shape),
            ],
            out_specs=whole(heads * rows, latent),
            scratch_shapes=[pltpu.VMEM((pages * page_len, LANES), jnp.float32)],
        ),
        out_shape=jax.ShapeDtypeStruct((heads * rows, latent), jnp.bfloat16),
        compiler_params=pltpu.CompilerParams(vmem_limit_bytes=24 * MIB),
        name="attend",
    )(
        block.reshape(1).astype(jnp.int32),
        page_table,
        lengths.reshape(rows, 1),
        query_latent,
        query_rope,
        cache_latent,
        cache_rope,
    )


def project_kernel(parts, value_ref, proj_ref, *refs):
    latents, (out_refs, scratch) = refs[:parts], (refs[parts : 2 * parts], refs[2 * parts :])
    value, proj, value_sem, proj_sem = scratch
    heads, latent, width = value_ref.shape
    rows = latents[0].shape[0] // heads
    chunks, chunk = proj.shape[0], proj.shape[2]
    value_copy = pltpu.make_async_copy(value_ref, value, value_sem)
    value_copy.start()
    copies = []
    for step in range(chunks):
        copies.append(
            pltpu.make_async_copy(
                proj_ref.at[:, pl.ds(step * chunk, chunk)], proj.at[step], proj_sem.at[step]
            )
        )
        copies[-1].start()
    value_copy.wait()
    outs = []
    for head in range(heads):
        both = jnp.concatenate(
            [ref[head * rows : (head + 1) * rows, :] for ref in latents], axis=0
        )
        outs.append(
            jnp.dot(both, value[head], preferred_element_type=jnp.float32).astype(jnp.bfloat16)
        )
    head_out = jnp.concatenate(outs, axis=1)
    for step in range(chunks):
        copies[step].wait()
        terms = jnp.dot(head_out, proj[step], preferred_element_type=jnp.float32)
        for part, out in enumerate(out_refs):
            out[:, step * chunk : (step + 1) * chunk] = terms[
                part * rows : (part + 1) * rows
            ].astype(out.dtype)


def project(latents, out_types, value_up, out_proj):
    heads, latent, width = value_up.shape
    rows = latents[0].shape[0] // heads
    model = out_proj.shape[1]
    chunks = 4
    vmem = pl.BlockSpec(memory_space=pltpu.VMEM)
    hbm = pl.BlockSpec(memory_space=pl.ANY)
    return pl.pallas_call(
        functools.partial(project_kernel, len(latents)),
        in_specs=[hbm, hbm] + [vmem] * len(latents),
        out_specs=[vmem] * len(latents),
        out_shape=[jax.ShapeDtypeStruct((rows, model), kind) for kind in out_types],
        scratch_shapes=[
            pltpu.VMEM(value_up.shape, jnp.bfloat16),
            pltpu.VMEM((chunks, out_proj.shape[0], model // chunks), jnp.bfloat16),
            pltpu.SemaphoreType.DMA,
            pltpu.SemaphoreType.DMA((chunks,)),
        ],
        compiler_params=pltpu.CompilerParams(vmem_limit_bytes=24 * MIB),
        name="project",
    )(value_up, out_proj, *latents)


def expert_kernel(blocks, slot_ref, gate_ref, up_ref, down_ref, *refs):
    inputs, outs, scratch = refs[:blocks], refs[blocks : 2 * blocks], refs[2 * blocks :]
    gate, up, down, act, sems = scratch
    hidden_units, model = gate.shape
    lots = [(0, 256), (256, 256), (512, hidden_units - 512)] if hidden_units > 512 else [
        (0, hidden_units)
    ]
    columns = 512
    copies = []
    for number, (begin, size) in enumerate(lots):
        for kind, (source, target) in enumerate(((gate_ref, gate), (up_ref, up))):
            where = pl.ds(begin, size)
            copies.append(
                pltpu.make_async_copy(source.at[where], target.at[where], sems.at[kind, number])
            )
            copies[-1].start()
    down_copy = pltpu.make_async_copy(down_ref, down, sems.at[2, 0])
    down_copy.start()
    rows = jnp.concatenate([ref[:, :model] for ref in inputs], axis=0)
    tails = jnp.concatenate([ref[:, model:] for ref in inputs], axis=0).astype(jnp.float32)
    lane = lax.broadcasted_iota(jnp.int32, tails.shape, 1)
    half = tails.shape[1] // 2
    slot = slot_ref[0]
    mine = (lane == slot) | (lane == slot + half)
    weight = jnp.sum(jnp.where(mine, tails, 0.0), axis=1, keepdims=True)
    for number, (begin, size) in enumerate(lots):
        copies[2 * number].wait()
        gate_values = lax.dot_general(
            rows, gate[begin : begin + size], NT, preferred_element_type=jnp.float32
        )
        copies[2 * number + 1].wait()
        up_values = lax.dot_general(
            rows, up[begin : begin + size], NT, preferred_element_type=jnp.float32
        )
        act[:, begin : begin + size] = (
            gate_values / (1.0 + jnp.exp(-gate_values)) * up_values
        ).astype(jnp.bfloat16)
    down_copy.wait()
    active = act[...]
    for begin in range(0, model, columns):
        terms = jnp.dot(
            active, down[:, begin : begin + columns], preferred_element_type=jnp.float32
        )
        terms = terms * weight
        at = 0
        for out in outs:
            out[:, begin : begin + columns] = terms[at : at + out.shape[0]].astype(out.dtype)
            at += out.shape[0]


def run_experts(slot, gate, up, down, inputs, out_types):
    hidden_units, model = gate.shape
    total = sum(block.shape[0] for block in inputs)
    vmem = pl.BlockSpec(memory_space=pltpu.VMEM)
    hbm = pl.BlockSpec(memory_space=pl.ANY)
    return pl.pallas_call(
        functools.partial(expert_kernel, len(inputs)),
        in_specs=[pl.BlockSpec(memory_space=pltpu.SMEM), hbm, hbm, hbm] + [vmem] * len(inputs),
        out_specs=[vmem] * len(inputs),
        out_shape=[
            jax.ShapeDtypeStruct((block.shape[0], model), kind)
            for block, kind in zip(inputs, out_types)
        ],
        scratch_shapes=[
            pltpu.VMEM(gate.shape, jnp.bfloat16),
            pltpu.VMEM(up.shape, jnp.bfloat16),
            pltpu.VMEM(down.shape, jnp.bfloat16),
            pltpu.VMEM((total, hidden_units), jnp.bfloat16),
            pltpu.SemaphoreType.DMA((3, 3)),
        ],
        compiler_params=pltpu.CompilerParams(vmem_limit_bytes=40 * MIB),
        name="experts",
    )(slot.reshape(1).astype(jnp.int32), gate, up, down, *inputs)


def shared_terms(rows, shared_gate, shared_up, shared_down):
    act = (
        jax.nn.silu(jnp.dot(rows, shared_gate, preferred_element_type=jnp.float32))
        * jnp.dot(rows, shared_up, preferred_element_type=jnp.float32)
    ).astype(jnp.bfloat16)
    return jnp.dot(act, shared_down, preferred_element_type=jnp.float32)


def exchanges(groups, replicas):
    lines = replicas

    def flip(dz=0, dy=0, dc=0, dx=0):
        pairs = []
        for group in range(groups):
            z, y, core = group // (2 * lines), group // 2 % lines, group % 2
            other = ((z ^ dz) * lines + (y ^ dy)) * 2 + (core ^ dc)
            for rep in range(replicas):
                pairs.append((group * replicas + rep, other * replicas + (rep ^ dx)))
        return pairs

    return lambda value, **by: lax.ppermute(value, AXES, flip(**by))


def route_columns(routes, route_weight, placement):
    experts = placement.shape[0]
    ids = jnp.arange(experts, dtype=jnp.int32)
    slots = jnp.sum(jnp.where(routes[:, :, None] == ids, placement, 0), axis=2)
    table = jnp.sum(jnp.where(slots[:, :, None] == ids, route_weight[:, :, None], 0.0), axis=1)
    half = -(-experts // 64) * 64
    table = jnp.pad(table, ((0, 0), (0, half - experts)))
    high = table.astype(jnp.bfloat16)
    low = (table - high.astype(jnp.float32)).astype(jnp.bfloat16)
    return jnp.concatenate([high, low], axis=1)


def finish(mixed, norm_gain):
    inverse = lax.rsqrt(jnp.mean(mixed * mixed, axis=1, keepdims=True) + EPSILON)
    return (mixed * inverse * norm_gain).astype(jnp.bfloat16)


def per_device(
    residual,
    query_latent,
    query_rope,
    cache_latent,
    cache_rope,
    page_table,
    lengths,
    value_up,
    out_proj,
    routes,
    route_weight,
    placement,
    expert_gate,
    expert_up,
    expert_down,
    shared_gate,
    shared_up,
    shared_down,
    norm_gain,
):
    replicas = lax.axis_size("rep")
    groups = lax.axis_size("ep")
    rep = lax.axis_index("rep")
    slot = lax.axis_index("ep")
    own = page_table.shape[0]
    heads = value_up.shape[0]
    own_rows = lambda value: lax.dynamic_slice_in_dim(value, rep * own, own, 0)
    caches = (query_latent, query_rope, cache_latent, cache_rope, page_table, lengths)
    columns = route_columns(own_rows(routes), own_rows(route_weight), placement)
    own_residual = own_rows(residual)
    gate = expert_gate[0].T
    up = expert_up[0].T
    down = expert_down[0]
    small = replicas == 2 and groups == 16

    if small:
        swap = exchanges(groups, replicas)
        away = attend(1 - rep, heads, *caches)
        arrived = swap(away, dx=1)
        kept = attend(rep, heads, *caches)
        send, keep = project([arrived, kept], [jnp.bfloat16, jnp.float32], value_up, out_proj)
        attended = (keep + swap(send, dx=1).astype(jnp.float32)).astype(jnp.bfloat16)
    else:
        latents = attend(jnp.int32(0), heads * replicas, *caches)
        latents = lax.all_to_all(latents, "rep", 0, 0, tiled=True).reshape(replicas, -1, latents.shape[1])
        terms = project(
            [latents[i] for i in range(replicas)], [jnp.bfloat16] * replicas, value_up, out_proj
        )
        attended = lax.psum_scatter(
            jnp.concatenate(terms, axis=0), "rep", scatter_dimension=0, tiled=True
        )
    hidden = (own_residual.astype(jnp.float32) + attended.astype(jnp.float32)).astype(jnp.bfloat16)
    model = hidden.shape[1]
    block = jnp.concatenate([hidden, columns], axis=1)

    if not small:
        every = lax.all_gather(block, AXES, axis=0, tiled=True)
        inputs = [every[at : at + 512] for at in range(0, every.shape[0], 512)]
        terms = []
        for piece in inputs:
            terms += run_experts(slot, gate, up, down, [piece], [jnp.bfloat16])
        mine = lax.dynamic_slice_in_dim(every, slot * replicas * own, replicas * own, 0)[:, :model]
        shared = shared_terms(mine, shared_gate, shared_up, shared_down).astype(jnp.bfloat16)
        total = lax.psum_scatter(
            jnp.concatenate(terms, axis=0), AXES, scatter_dimension=0, tiled=True
        ).astype(jnp.float32)
        total = total + lax.psum_scatter(
            shared, "rep", scatter_dimension=0, tiled=True
        ).astype(jnp.float32)
        return finish(hidden.astype(jnp.float32) + total, norm_gain)

    line = [block] + [swap(block, dz=step) for step in (1, 2, 3)]
    column = jnp.concatenate(line, axis=0)
    planes = [column, swap(column, dx=1), swap(column, dy=1), swap(column, dx=1, dy=1)]
    others = [swap(plane, dc=1) for plane in planes]
    terms = run_experts(
        slot, gate, up, down, others + planes, [jnp.bfloat16] * 4 + [jnp.bfloat16] * 4
    )
    pair = jnp.concatenate([planes[1][:own, :model], hidden], axis=0)
    shared = shared_terms(pair, shared_gate, shared_up, shared_down)
    crossed = [swap(term, dc=1) for term in terms[:4]]
    sums = [
        mine.astype(jnp.float32) + other.astype(jnp.float32)
        for mine, other in zip(terms[4:], crossed)
    ]
    sums[1] = sums[1] + jnp.pad(shared[:own], ((0, 3 * own), (0, 0)))
    total = sums[0]
    for value, by in zip(sums[1:], (dict(dx=1), dict(dy=1), dict(dx=1, dy=1))):
        total = total + swap(value.astype(jnp.bfloat16), **by).astype(jnp.float32)
    mixed = hidden.astype(jnp.float32) + shared[own:] + total[:own]
    for step in (1, 2, 3):
        piece = total[step * own : (step + 1) * own].astype(jnp.bfloat16)
        mixed = mixed + swap(piece, dz=step).astype(jnp.float32)
    return finish(mixed, norm_gain)


def solution(mesh):
    in_specs = (
        P("ep", None),
        P(("ep", "rep"), None),
        P(("ep", "rep"), None),
        P(("ep", "rep"), None, None),
        P(("ep", "rep"), None),
        P(("ep", "rep"), None),
        P(("ep", "rep")),
        P("rep", None, None),
        P("rep", None),
        P("ep", None),
        P("ep", None),
        P(),
        P("ep", None, "rep"),
        P("ep", None, "rep"),
        P("ep", "rep", None),
        P(None, "rep"),
        P(None, "rep"),
        P("rep", None),
        P(),
    )
    out_specs = P(("ep", "rep"), None)
    return jax.shard_map(
        per_device, mesh=mesh, in_specs=in_specs, out_specs=out_specs, check_vma=False
    )
```

```python
import functools
import math

import jax
import jax.numpy as jnp
from jax import lax
from jax.experimental import pallas as pl
from jax.experimental.pallas import tpu as pltpu
from jax.sharding import PartitionSpec as P

ROPE = 64
VHEAD = 128
LANES = 128
EPSILON = 1e-06
AXES = ("ep", "rep")
MIB = 1024 * 1024
NT = (((1,), (1,)), ((), ()))


def in_hbm(value):
    return pltpu.with_memory_space_constraint(value, pltpu.HBM)


def attend_heads(query_ref, rot_ref, key_lat, key_rot, count, out_ref, before_latent, before_keys):
    rows, keys = count.shape
    latent = key_lat.shape[1]
    heads = out_ref.shape[0] // rows
    low = lax.broadcasted_iota(jnp.int32, (rows, LANES), 1) < ROPE
    rot_parts = []
    for head in range(heads):
        pair = rot_ref[:, head // 2 * LANES : (head // 2 + 1) * LANES].astype(jnp.float32)
        if head % 2:
            pair = pltpu.roll(pair, ROPE, 1)
        rot_parts.append(jnp.where(low, pair, 0.0).astype(jnp.bfloat16))
    rot = jnp.concatenate(rot_parts, axis=0)
    scores = lax.dot_general(rot, key_rot[...], NT, preferred_element_type=jnp.float32)
    before_latent()
    query = jnp.concatenate(
        [query_ref[:, head * latent : (head + 1) * latent] for head in range(heads)], axis=0
    )
    before_keys()
    scores = (
        lax.dot_general(query, key_lat[...], NT, preferred_element_type=jnp.float32) + scores
    ) * (1.0 / math.sqrt(VHEAD + ROPE))
    scores = scores.reshape(heads, rows, keys)
    counts = count[...][None]
    masked = jnp.where(counts > 0.0, scores, -jnp.inf)
    peak = jnp.max(masked, axis=2, keepdims=True)
    expons = jnp.exp(masked - peak) * counts
    probs = (expons / jnp.sum(expons, axis=2, keepdims=True)).astype(jnp.bfloat16)
    out_ref[...] = jnp.dot(
        probs.reshape(heads * rows, keys), key_lat[...], preferred_element_type=jnp.float32
    ).astype(jnp.bfloat16)


def head_columns(ref, head_block, width):
    return ref.at[:, pl.ds(pl.multiple_of(head_block * width, LANES), width)]


def attend_kernel(
    block_ref,
    lengths_hbm,
    table_hbm,
    query_hbm,
    rot_hbm,
    pages_hbm,
    rope_hbm,
    out_ref,
    key_lat,
    key_rot,
    count,
    lengths_ref,
    table_ref,
    query_ref,
    rot_ref,
    rope_ref,
    keys_rope,
    sems,
):
    rows, span = table_ref.shape
    pages, page_len, latent = pages_hbm.shape
    keys = pages * page_len
    copies = [
        pltpu.make_async_copy(source, target, sems.at[number])
        for number, (source, target) in enumerate(
            (
                (rope_hbm, rope_ref),
                (table_hbm, table_ref),
                (lengths_hbm, lengths_ref),
                (head_columns(rot_hbm, block_ref[0], rot_ref.shape[1]), rot_ref),
                (head_columns(query_hbm, block_ref[0], query_ref.shape[1]), query_ref),
                (pages_hbm, key_lat.reshape(pages, page_len, latent)),
            )
        )
    ]
    for copy in copies:
        copy.start()
    copies[0].wait()
    for pair in range(page_len // 2):
        both = rope_ref[:, pair * LANES : (pair + 1) * LANES].astype(jnp.float32)
        keys_rope[pl.ds(2 * pair, pages, stride=page_len), :] = both
        keys_rope[pl.ds(2 * pair + 1, pages, stride=page_len), :] = pltpu.roll(both, ROPE, 1)
    key_rot[...] = keys_rope[...].astype(jnp.bfloat16)
    copies[1].wait()
    copies[2].wait()
    row_ids = lax.broadcasted_iota(jnp.int32, (rows, LANES), 0)
    lengths = jnp.zeros((rows, LANES), jnp.int32)
    for row in range(rows):
        lengths = jnp.where(row_ids == row, lengths_ref[row], lengths)
    lengths = lengths[:, :1]
    key_ids = lax.broadcasted_iota(jnp.int32, (rows, keys), 1)
    page_of, slot_of = key_ids // page_len, key_ids % page_len
    total = jnp.zeros((rows, keys), jnp.float32)
    for step in range(span):
        live = (table_ref[:, step : step + 1] == page_of) & (slot_of + step * page_len < lengths)
        total = total + jnp.where(live, 1.0, 0.0)
    count[...] = total
    copies[3].wait()
    attend_heads(
        query_ref, rot_ref, key_lat, key_rot, count, out_ref, copies[4].wait, copies[5].wait
    )


def attend(block, heads, query_latent, query_rope, cache_latent, cache_rope, page_table, lengths):
    rows = page_table.shape[0]
    pages, page_len, latent = cache_latent.shape
    keys = pages * page_len
    operands = (lengths, page_table, query_latent, query_rope, cache_latent, cache_rope)
    out, *prepared = pl.pallas_call(
        attend_kernel,
        in_specs=[pl.BlockSpec(memory_space=pltpu.SMEM)]
        + [pl.BlockSpec(memory_space=pl.ANY)] * len(operands),
        out_specs=[pl.BlockSpec(memory_space=pltpu.VMEM)] * 4,
        out_shape=[
            pltpu.VMEM((heads * rows, latent), jnp.bfloat16),
            pltpu.VMEM((keys, latent), jnp.bfloat16),
            pltpu.VMEM((keys, LANES), jnp.bfloat16),
            pltpu.VMEM((rows, keys), jnp.float32),
        ],
        scratch_shapes=[
            pltpu.SMEM(lengths.shape, jnp.int32),
            pltpu.VMEM(page_table.shape, jnp.int32),
            pltpu.VMEM((rows, heads * latent), jnp.bfloat16),
            pltpu.VMEM((rows, heads * ROPE), jnp.bfloat16),
            pltpu.VMEM(cache_rope.shape, jnp.bfloat16),
            pltpu.VMEM((keys, LANES), jnp.float32),
            pltpu.SemaphoreType.DMA((len(operands),)),
        ],
        compiler_params=pltpu.CompilerParams(vmem_limit_bytes=16 * MIB),
        cost_estimate=pl.CostEstimate(
            flops=4 * heads * rows * keys * latent,
            bytes_accessed=4 * MIB,
            transcendentals=heads * rows * keys,
        ),
        name="attend",
    )(block.reshape(1).astype(jnp.int32), *[in_hbm(value) for value in operands])
    return out, prepared


def attend_more_kernel(
    staged, block_ref, key_lat, key_rot, count, query_hbm, rot_hbm, *refs
):
    sources, (out_ref, *targets) = refs[:staged], refs[staged : 2 * staged + 1]
    query_ref, rot_ref, sems = refs[2 * staged + 1 :]
    copies = [
        pltpu.make_async_copy(source, target, sems.at[number])
        for number, (source, target) in enumerate(
            (
                (head_columns(rot_hbm, block_ref[0], rot_ref.shape[1]), rot_ref),
                (head_columns(query_hbm, block_ref[0], query_ref.shape[1]), query_ref),
                *zip(sources, targets),
            )
        )
    ]
    for copy in copies:
        copy.start()
    copies[0].wait()
    attend_heads(
        query_ref, rot_ref, key_lat, key_rot, count, out_ref, copies[1].wait, lambda: None
    )
    for copy in copies[2:]:
        copy.wait()


def attend_more(block, heads, prepared, query_latent, query_rope, values):
    key_lat, key_rot, count = prepared
    rows, keys = count.shape
    latent = key_lat.shape[1]
    vmem = pl.BlockSpec(memory_space=pltpu.VMEM)
    anywhere = pl.BlockSpec(memory_space=pl.ANY)
    return pl.pallas_call(
        functools.partial(attend_more_kernel, len(values)),
        in_specs=[pl.BlockSpec(memory_space=pltpu.SMEM)] + [vmem] * 3 + [anywhere] * (2 + len(values)),
        out_specs=[vmem] * (1 + len(values)),
        out_shape=[pltpu.VMEM((heads * rows, latent), jnp.bfloat16)]
        + [pltpu.VMEM(value.shape, value.dtype) for value in values],
        scratch_shapes=[
            pltpu.VMEM((rows, heads * latent), jnp.bfloat16),
            pltpu.VMEM((rows, heads * ROPE), jnp.bfloat16),
            pltpu.SemaphoreType.DMA((2 + len(values),)),
        ],
        compiler_params=pltpu.CompilerParams(vmem_limit_bytes=16 * MIB),
        cost_estimate=pl.CostEstimate(
            flops=4 * heads * rows * keys * latent,
            bytes_accessed=8 * MIB,
            transcendentals=heads * rows * keys,
        ),
        name="attend_more",
    )(
        block.reshape(1).astype(jnp.int32),
        *prepared,
        *[in_hbm(value) for value in (query_latent, query_rope, *values)],
    )


def project_kernel(parts, value_ref, proj_ref, *refs):
    latents, out_refs = refs[:parts], refs[parts : 2 * parts]
    heads, latent, width = value_ref.shape
    rows = latents[0].shape[0] // heads
    outs = []
    for head in range(heads):
        both = jnp.concatenate(
            [ref[head * rows : (head + 1) * rows, :] for ref in latents], axis=0
        )
        outs.append(
            jnp.dot(both, value_ref[head], preferred_element_type=jnp.float32).astype(jnp.bfloat16)
        )
    head_out = jnp.concatenate(outs, axis=1)
    chunk = 512
    for begin in range(0, proj_ref.shape[1], chunk):
        terms = jnp.dot(
            head_out, proj_ref[:, begin : begin + chunk], preferred_element_type=jnp.float32
        )
        for part, out in enumerate(out_refs):
            out[:, begin : begin + chunk] = terms[part * rows : (part + 1) * rows].astype(out.dtype)


def project(latents, out_types, value_up, out_proj):
    heads, latent, width = value_up.shape
    rows = latents[0].shape[0] // heads
    model = out_proj.shape[1]
    vmem = pl.BlockSpec(memory_space=pltpu.VMEM)
    return pl.pallas_call(
        functools.partial(project_kernel, len(latents)),
        in_specs=[vmem] * (2 + len(latents)),
        out_specs=[vmem] * len(latents),
        out_shape=[pltpu.VMEM((rows, model), kind) for kind in out_types],
        compiler_params=pltpu.CompilerParams(vmem_limit_bytes=16 * MIB),
        cost_estimate=pl.CostEstimate(
            flops=2 * len(latents) * rows * out_proj.size,
            bytes_accessed=2 * (value_up.size + out_proj.size),
            transcendentals=0,
        ),
        name="project",
    )(value_up, out_proj, *latents)


def stage_kernel(count, after_ref, *refs):
    del after_ref
    sources, targets, (token, sems) = refs[:count], refs[count : 2 * count], refs[2 * count :]
    copies = [
        pltpu.make_async_copy(source, target, sems.at[number])
        for number, (source, target) in enumerate(zip(sources, targets))
    ]
    for copy in copies:
        copy.start()
    token[...] = jnp.zeros_like(token)
    for copy in copies:
        copy.wait()


def stage(after, values):
    anywhere = pl.BlockSpec(memory_space=pl.ANY)
    *staged, token = pl.pallas_call(
        functools.partial(stage_kernel, len(values)),
        in_specs=[anywhere] * (1 + len(values)),
        out_specs=[pl.BlockSpec(memory_space=pltpu.VMEM)] * (1 + len(values)),
        out_shape=[pltpu.VMEM(value.shape, value.dtype) for value in values]
        + [jax.ShapeDtypeStruct((8, LANES), jnp.float32)],
        scratch_shapes=[pltpu.SemaphoreType.DMA((len(values),))],
        compiler_params=pltpu.CompilerParams(vmem_limit_bytes=16 * MIB),
        cost_estimate=pl.CostEstimate(
            flops=0,
            bytes_accessed=2 * sum(value.size * value.dtype.itemsize for value in values),
            transcendentals=0,
        ),
        name="stage",
    )(after, *[in_hbm(value) for value in values])
    return staged, token


def lots_of(units):
    return [(begin, min(256, units - begin)) for begin in range(0, units, 256)]


def activate(rows, gate, up):
    gate_values = lax.dot_general(rows, gate, NT, preferred_element_type=jnp.float32)
    up_values = lax.dot_general(rows, up, NT, preferred_element_type=jnp.float32)
    return (gate_values / (1.0 + jnp.exp(-gate_values)) * up_values).astype(jnp.bfloat16)


def expert_kernel(blocks, slot_ref, after_ref, gate_ref, up_ref, down_ref, *refs):
    del after_ref
    inputs, outs, (rows, act) = refs[:blocks], refs[blocks : 2 * blocks], refs[2 * blocks :]
    units, model = gate_ref.shape
    columns = 512
    slot = slot_ref[0]
    weights, at = [], 0
    for ref in inputs:
        rows[at : at + ref.shape[0], :] = ref[:, :model]
        at += ref.shape[0]
        tail = ref[:, model:].astype(jnp.float32)
        lane = lax.broadcasted_iota(jnp.int32, tail.shape, 1)
        mine = (lane == slot) | (lane == slot + tail.shape[1] // 2)
        weights.append(jnp.sum(jnp.where(mine, tail, 0.0), axis=1, keepdims=True))
    weight = jnp.concatenate(weights, axis=0)
    for begin, size in lots_of(units):
        lot = pl.ds(begin, size)
        act[:, begin : begin + size] = activate(rows[...], gate_ref[lot, :], up_ref[lot, :])
    for begin in range(0, model, columns):
        terms = weight * jnp.dot(
            act[...], down_ref[:, begin : begin + columns], preferred_element_type=jnp.float32
        )
        at = 0
        for out in outs:
            out[:, begin : begin + columns] = terms[at : at + out.shape[0]].astype(out.dtype)
            at += out.shape[0]


def run_experts(slot, after, gate, up, down, inputs):
    units, model = gate.shape
    total = sum(block.shape[0] for block in inputs)
    vmem = pl.BlockSpec(memory_space=pltpu.VMEM)
    return pl.pallas_call(
        functools.partial(expert_kernel, len(inputs)),
        in_specs=[pl.BlockSpec(memory_space=pltpu.SMEM), pl.BlockSpec(memory_space=pl.ANY)]
        + [vmem] * (3 + len(inputs)),
        out_specs=[vmem] * len(inputs),
        out_shape=[pltpu.VMEM((block.shape[0], model), jnp.bfloat16) for block in inputs],
        scratch_shapes=[
            pltpu.VMEM((total, model), jnp.bfloat16),
            pltpu.VMEM((total, units), jnp.bfloat16),
        ],
        compiler_params=pltpu.CompilerParams(vmem_limit_bytes=28 * MIB),
        cost_estimate=pl.CostEstimate(
            flops=6 * total * units * model,
            bytes_accessed=6 * units * model + 4 * total * model,
            transcendentals=total * units,
        ),
        name="experts",
    )(slot, after, gate, up, down, *inputs)


def shared_kernel(gate_hbm, up_hbm, down_hbm, after_ref, rows_ref, out_ref, gate, up, down, act, sems):
    del after_ref
    units, model = gate.shape
    lots, columns = lots_of(units), 1024
    copies = []
    for number, (begin, size) in enumerate(lots):
        for kind, (source, target) in enumerate(((gate_hbm, gate), (up_hbm, up))):
            lot = pl.ds(begin, size)
            copies.append(
                pltpu.make_async_copy(source.at[lot], target.at[lot], sems.at[kind, number])
            )
    copies.append(pltpu.make_async_copy(down_hbm, down, sems.at[2, 0]))
    for copy in copies:
        copy.start()
    for number, (begin, size) in enumerate(lots):
        copies[2 * number].wait()
        copies[2 * number + 1].wait()
        lot = pl.ds(begin, size)
        act[:, begin : begin + size] = activate(rows_ref[...], gate[lot, :], up[lot, :])
    copies[-1].wait()
    for begin in range(0, model, columns):
        out_ref[:, begin : begin + columns] = jnp.dot(
            act[...], down[:, begin : begin + columns], preferred_element_type=jnp.float32
        )


def run_shared(after, rows, gate, up, down):
    units, model = gate.shape
    vmem = pl.BlockSpec(memory_space=pltpu.VMEM)
    anywhere = pl.BlockSpec(memory_space=pl.ANY)
    return pl.pallas_call(
        shared_kernel,
        in_specs=[anywhere] * 4 + [vmem],
        out_specs=vmem,
        out_shape=pltpu.VMEM((rows.shape[0], model), jnp.float32),
        scratch_shapes=[
            pltpu.VMEM(gate.shape, jnp.bfloat16),
            pltpu.VMEM(up.shape, jnp.bfloat16),
            pltpu.VMEM(down.shape, jnp.bfloat16),
            pltpu.VMEM((rows.shape[0], units), jnp.bfloat16),
            pltpu.SemaphoreType.DMA((3, len(lots_of(units)))),
        ],
        compiler_params=pltpu.CompilerParams(vmem_limit_bytes=24 * MIB),
        cost_estimate=pl.CostEstimate(
            flops=6 * rows.shape[0] * units * model,
            bytes_accessed=12 * units * model,
            transcendentals=rows.shape[0] * units,
        ),
        name="shared",
    )(*[in_hbm(value) for value in (gate, up, down)], after, rows)


def exchanges(groups, replicas):
    lines, depth = replicas, groups // (2 * replicas)

    def moves(dz=0, dy=0, dc=0, dx=0):
        pairs = []
        for group in range(groups):
            z, y, core = group // (2 * lines), group // 2 % lines, group % 2
            other = ((z + dz) % depth * lines + (y ^ dy)) * 2 + (core ^ dc)
            for rep in range(replicas):
                pairs.append((group * replicas + rep, other * replicas + (rep ^ dx)))
        return pairs

    return lambda value, **by: lax.ppermute(value, AXES, moves(**by))


def route_columns(routes, route_weight, placement):
    experts = placement.shape[0]
    ids = jnp.arange(experts, dtype=jnp.int32)
    slots = jnp.sum(jnp.where(routes[:, :, None] == ids, placement, 0), axis=2)
    table = jnp.sum(jnp.where(slots[:, :, None] == ids, route_weight[:, :, None], 0.0), axis=1)
    half = -(-experts // 64) * 64
    table = jnp.pad(table, ((0, 0), (0, half - experts)))
    high = table.astype(jnp.bfloat16)
    low = (table - high.astype(jnp.float32)).astype(jnp.bfloat16)
    return jnp.concatenate([high, low], axis=1)


def enter(attended, own_rows, routes, route_weight, placement, residual):
    attended = attended.astype(jnp.bfloat16).astype(jnp.float32)
    hidden = (own_rows(residual).astype(jnp.float32) + attended).astype(jnp.bfloat16)
    columns = route_columns(own_rows(routes), own_rows(route_weight), placement)
    return jnp.concatenate([hidden, columns], axis=1), hidden


def exchange_experts(swap, block, hidden, slot, weights, shared):
    own, model = hidden.shape
    directions = (dict(dx=1), dict(dy=1), dict(dx=1, dy=1))
    line = [block] + [swap(block, dz=step) for step in (1, 2, 3)]
    column = jnp.concatenate(line, axis=0)
    column, slot = lax.optimization_barrier((column, slot))
    planes = [swap(column, **by) for by in directions]
    other = swap(column, dc=1)
    weights, token = stage(column, weights)
    planes, other, token = lax.optimization_barrier((planes, other, token))
    first = run_experts(slot, token, *weights, [column, *planes[:2], other])
    others = [swap(plane, dc=1) for plane in planes]
    last = run_experts(slot, token, *weights, [*others[:2], planes[2], others[2]])
    kept = [*first[:3], last[2]]
    crossed = [swap(term, dc=1) for term in (first[3], last[0], last[1], last[3])]
    sums = [
        mine.astype(jnp.float32) + term.astype(jnp.float32) for mine, term in zip(kept, crossed)
    ]
    returned = [
        swap(value.astype(jnp.bfloat16), **by) for value, by in zip(sums[1:], directions)
    ]
    pair = jnp.concatenate([planes[0][:own, :model], hidden], axis=0)
    own_terms = run_shared(last[0], pair, *shared)
    away = swap(own_terms[:own].astype(jnp.bfloat16), dx=1)
    total = sums[0]
    for value in returned:
        total = total + value.astype(jnp.float32)
    mixed = hidden.astype(jnp.float32) + own_terms[own:] + total[:own]
    for step in (1, 2, 3):
        piece = total[step * own : (step + 1) * own].astype(jnp.bfloat16)
        mixed = mixed + swap(piece, dz=-step).astype(jnp.float32)
    return mixed, away.astype(jnp.float32)


def finish(mixed, norm_gain):
    inverse = lax.rsqrt(jnp.mean(mixed * mixed, axis=1, keepdims=True) + EPSILON)
    return (mixed * inverse * norm_gain).astype(jnp.bfloat16)


def per_device(
    residual,
    query_latent,
    query_rope,
    cache_latent,
    cache_rope,
    page_table,
    lengths,
    value_up,
    out_proj,
    routes,
    route_weight,
    placement,
    expert_gate,
    expert_up,
    expert_down,
    shared_gate,
    shared_up,
    shared_down,
    norm_gain,
):
    replicas = lax.axis_size("rep")
    groups = lax.axis_size("ep")
    rep = lax.axis_index("rep")
    slot = lax.axis_index("ep").reshape(1).astype(jnp.int32)
    own = page_table.shape[0]
    heads = value_up.shape[0]
    own_rows = lambda value: lax.dynamic_slice_in_dim(value, rep * own, own, 0)
    caches = (query_latent, query_rope, cache_latent, cache_rope, page_table, lengths)
    gate = expert_gate[0].T
    up = expert_up[0].T
    down = expert_down[0]
    shared = (shared_gate.T, shared_up.T, shared_down)
    routing = (routes, route_weight, placement, residual)

    if replicas == 2 and groups == 16:
        swap = exchanges(groups, replicas)
        away, prepared = attend(1 - rep, heads, *caches)
        arrived = swap(away, dx=1)
        kept, value_up, out_proj = attend_more(
            rep, heads, prepared, query_latent, query_rope, (value_up, out_proj)
        )
        send, keep = project([arrived, kept], [jnp.bfloat16, jnp.float32], value_up, out_proj)
        send, routing = lax.optimization_barrier((send, routing))
        block, hidden = enter(keep + swap(send, dx=1).astype(jnp.float32), own_rows, *routing)
        total, mixed_shared = exchange_experts(
            swap, block, hidden, slot, (gate, up, down), shared
        )
        return finish(total + mixed_shared, norm_gain)

    latents, _ = attend(jnp.int32(0), heads * replicas, *caches)
    latents = lax.all_to_all(latents, "rep", 0, 0, tiled=True)
    latents = latents.reshape(replicas, -1, latents.shape[1])
    terms = project(
        [latents[i] for i in range(replicas)], [jnp.bfloat16] * replicas, value_up, out_proj
    )
    attended = lax.psum_scatter(
        jnp.concatenate(terms, axis=0), "rep", scatter_dimension=0, tiled=True
    )
    block, hidden = enter(attended, own_rows, *routing)
    model = hidden.shape[1]
    every = lax.all_gather(block, AXES, axis=0, tiled=True)
    lot = min(512, every.shape[0])
    terms = [
        run_experts(slot, slot, gate, up, down, [every[at : at + lot]])[0]
        for at in range(0, every.shape[0], lot)
    ]
    mine = lax.dynamic_slice_in_dim(every, slot[0] * replicas * own, replicas * own, 0)[:, :model]
    own_terms = run_shared(mine, mine, *shared).astype(jnp.bfloat16)
    total = lax.psum_scatter(
        jnp.concatenate(terms, axis=0), AXES, scatter_dimension=0, tiled=True
    ).astype(jnp.float32)
    total = total + lax.psum_scatter(
        own_terms, "rep", scatter_dimension=0, tiled=True
    ).astype(jnp.float32)
    return finish(hidden.astype(jnp.float32) + total, norm_gain)


def solution(mesh):
    in_specs = (
        P("ep", None),
        P(("ep", "rep"), None),
        P(("ep", "rep"), None),
        P(("ep", "rep"), None, None),
        P(("ep", "rep"), None),
        P(("ep", "rep"), None),
        P(("ep", "rep")),
        P("rep", None, None),
        P("rep", None),
        P("ep", None),
        P("ep", None),
        P(),
        P("ep", None, "rep"),
        P("ep", None, "rep"),
        P("ep", "rep", None),
        P(None, "rep"),
        P(None, "rep"),
        P("rep", None),
        P(),
    )
    out_specs = P(("ep", "rep"), None)
    return jax.shard_map(
        per_device, mesh=mesh, in_specs=in_specs, out_specs=out_specs, check_vma=False
    )
```

```python
import functools
import math

import jax
import jax.numpy as jnp
from jax import lax
from jax.experimental import pallas as pl
from jax.experimental.pallas import tpu as pltpu
from jax.sharding import PartitionSpec as P

ROPE = 64
VHEAD = 128
LANES = 128
EPSILON = 1e-06
AXES = ("ep", "rep")
MIB = 1024 * 1024
NT = (((1,), (1,)), ((), ()))


def in_hbm(value):
    return pltpu.with_memory_space_constraint(value, pltpu.HBM)


def attend_heads(query_ref, rot_ref, key_lat, key_rot, count, out_ref, before_latent, before_keys):
    rows, keys = count.shape
    latent = key_lat.shape[1]
    heads = out_ref.shape[0] // rows
    low = lax.broadcasted_iota(jnp.int32, (rows, LANES), 1) < ROPE
    rot_parts = []
    for head in range(heads):
        pair = rot_ref[:, head // 2 * LANES : (head // 2 + 1) * LANES].astype(jnp.float32)
        if head % 2:
            pair = pltpu.roll(pair, ROPE, 1)
        rot_parts.append(jnp.where(low, pair, 0.0).astype(jnp.bfloat16))
    rot = jnp.concatenate(rot_parts, axis=0)
    scores = lax.dot_general(rot, key_rot[...], NT, preferred_element_type=jnp.float32)
    before_latent()
    query = jnp.concatenate(
        [query_ref[:, head * latent : (head + 1) * latent] for head in range(heads)], axis=0
    )
    before_keys()
    scores = (
        lax.dot_general(query, key_lat[...], NT, preferred_element_type=jnp.float32) + scores
    ) * (1.0 / math.sqrt(VHEAD + ROPE))
    scores = scores.reshape(heads, rows, keys)
    counts = count[...][None]
    masked = jnp.where(counts > 0.0, scores, -jnp.inf)
    peak = jnp.max(masked, axis=2, keepdims=True)
    expons = jnp.exp(masked - peak) * counts
    probs = (expons / jnp.sum(expons, axis=2, keepdims=True)).astype(jnp.bfloat16)
    out_ref[...] = jnp.dot(
        probs.reshape(heads * rows, keys), key_lat[...], preferred_element_type=jnp.float32
    ).astype(jnp.bfloat16)


def head_columns(ref, head_block, width):
    return ref.at[:, pl.ds(pl.multiple_of(head_block * width, LANES), width)]


def attend_kernel(
    block_ref,
    lengths_hbm,
    table_hbm,
    query_hbm,
    rot_hbm,
    pages_hbm,
    rope_hbm,
    out_ref,
    key_lat,
    key_rot,
    count,
    lengths_ref,
    table_ref,
    query_ref,
    rot_ref,
    rope_ref,
    keys_rope,
    sems,
):
    rows, span = table_ref.shape
    pages, page_len, latent = pages_hbm.shape
    keys = pages * page_len
    copies = [
        pltpu.make_async_copy(source, target, sems.at[number])
        for number, (source, target) in enumerate(
            (
                (rope_hbm, rope_ref),
                (table_hbm, table_ref),
                (lengths_hbm, lengths_ref),
                (head_columns(rot_hbm, block_ref[0], rot_ref.shape[1]), rot_ref),
                (head_columns(query_hbm, block_ref[0], query_ref.shape[1]), query_ref),
                (pages_hbm, key_lat.reshape(pages, page_len, latent)),
            )
        )
    ]
    for copy in copies:
        copy.start()
    copies[0].wait()
    for pair in range(page_len // 2):
        both = rope_ref[:, pair * LANES : (pair + 1) * LANES].astype(jnp.float32)
        keys_rope[pl.ds(2 * pair, pages, stride=page_len), :] = both
        keys_rope[pl.ds(2 * pair + 1, pages, stride=page_len), :] = pltpu.roll(both, ROPE, 1)
    key_rot[...] = keys_rope[...].astype(jnp.bfloat16)
    copies[1].wait()
    copies[2].wait()
    row_ids = lax.broadcasted_iota(jnp.int32, (rows, LANES), 0)
    lengths = jnp.zeros((rows, LANES), jnp.int32)
    for row in range(rows):
        lengths = jnp.where(row_ids == row, lengths_ref[row], lengths)
    lengths = lengths[:, :1]
    key_ids = lax.broadcasted_iota(jnp.int32, (rows, keys), 1)
    page_of, slot_of = key_ids // page_len, key_ids % page_len
    total = jnp.zeros((rows, keys), jnp.float32)
    for step in range(span):
        live = (table_ref[:, step : step + 1] == page_of) & (slot_of + step * page_len < lengths)
        total = total + jnp.where(live, 1.0, 0.0)
    count[...] = total
    copies[3].wait()
    attend_heads(
        query_ref, rot_ref, key_lat, key_rot, count, out_ref, copies[4].wait, copies[5].wait
    )


def attend(block, heads, query_latent, query_rope, cache_latent, cache_rope, page_table, lengths):
    rows = page_table.shape[0]
    pages, page_len, latent = cache_latent.shape
    keys = pages * page_len
    operands = (lengths, page_table, query_latent, query_rope, cache_latent, cache_rope)
    out, *prepared = pl.pallas_call(
        attend_kernel,
        in_specs=[pl.BlockSpec(memory_space=pltpu.SMEM)]
        + [pl.BlockSpec(memory_space=pl.ANY)] * len(operands),
        out_specs=[pl.BlockSpec(memory_space=pltpu.VMEM)] * 4,
        out_shape=[
            pltpu.VMEM((heads * rows, latent), jnp.bfloat16),
            pltpu.VMEM((keys, latent), jnp.bfloat16),
            pltpu.VMEM((keys, LANES), jnp.bfloat16),
            pltpu.VMEM((rows, keys), jnp.float32),
        ],
        scratch_shapes=[
            pltpu.SMEM(lengths.shape, jnp.int32),
            pltpu.VMEM(page_table.shape, jnp.int32),
            pltpu.VMEM((rows, heads * latent), jnp.bfloat16),
            pltpu.VMEM((rows, heads * ROPE), jnp.bfloat16),
            pltpu.VMEM(cache_rope.shape, jnp.bfloat16),
            pltpu.VMEM((keys, LANES), jnp.float32),
            pltpu.SemaphoreType.DMA((len(operands),)),
        ],
        compiler_params=pltpu.CompilerParams(vmem_limit_bytes=16 * MIB),
        cost_estimate=pl.CostEstimate(
            flops=4 * heads * rows * keys * latent,
            bytes_accessed=4 * MIB,
            transcendentals=heads * rows * keys,
        ),
        name="attend",
    )(block.reshape(1).astype(jnp.int32), *[in_hbm(value) for value in operands])
    return out, prepared


def attend_more_kernel(
    staged, block_ref, key_lat, key_rot, count, query_hbm, rot_hbm, *refs
):
    sources, (out_ref, *targets) = refs[:staged], refs[staged : 2 * staged + 1]
    query_ref, rot_ref, sems = refs[2 * staged + 1 :]
    copies = [
        pltpu.make_async_copy(source, target, sems.at[number])
        for number, (source, target) in enumerate(
            (
                (head_columns(rot_hbm, block_ref[0], rot_ref.shape[1]), rot_ref),
                (head_columns(query_hbm, block_ref[0], query_ref.shape[1]), query_ref),
                *zip(sources, targets),
            )
        )
    ]
    for copy in copies:
        copy.start()
    copies[0].wait()
    attend_heads(
        query_ref, rot_ref, key_lat, key_rot, count, out_ref, copies[1].wait, lambda: None
    )
    for copy in copies[2:]:
        copy.wait()


def attend_more(block, heads, prepared, query_latent, query_rope, values):
    key_lat, key_rot, count = prepared
    rows, keys = count.shape
    latent = key_lat.shape[1]
    vmem = pl.BlockSpec(memory_space=pltpu.VMEM)
    anywhere = pl.BlockSpec(memory_space=pl.ANY)
    return pl.pallas_call(
        functools.partial(attend_more_kernel, len(values)),
        in_specs=[pl.BlockSpec(memory_space=pltpu.SMEM)] + [vmem] * 3 + [anywhere] * (2 + len(values)),
        out_specs=[vmem] * (1 + len(values)),
        out_shape=[pltpu.VMEM((heads * rows, latent), jnp.bfloat16)]
        + [pltpu.VMEM(value.shape, value.dtype) for value in values],
        scratch_shapes=[
            pltpu.VMEM((rows, heads * latent), jnp.bfloat16),
            pltpu.VMEM((rows, heads * ROPE), jnp.bfloat16),
            pltpu.SemaphoreType.DMA((2 + len(values),)),
        ],
        compiler_params=pltpu.CompilerParams(vmem_limit_bytes=16 * MIB),
        cost_estimate=pl.CostEstimate(
            flops=4 * heads * rows * keys * latent,
            bytes_accessed=8 * MIB,
            transcendentals=heads * rows * keys,
        ),
        name="attend_more",
    )(
        block.reshape(1).astype(jnp.int32),
        *prepared,
        *[in_hbm(value) for value in (query_latent, query_rope, *values)],
    )


def project_kernel(value_ref, proj_ref, *refs):
    latents, out_ref = refs[:-1], refs[-1]
    heads, latent, width = value_ref.shape
    rows = latents[0].shape[0] // heads
    outs = []
    for head in range(heads):
        both = jnp.concatenate(
            [ref[head * rows : (head + 1) * rows, :] for ref in latents], axis=0
        )
        outs.append(
            jnp.dot(both, value_ref[head], preferred_element_type=jnp.float32).astype(jnp.bfloat16)
        )
    head_out = jnp.concatenate(outs, axis=1)
    chunk = 512
    for begin in range(0, proj_ref.shape[1], chunk):
        out_ref[:, begin : begin + chunk] = jnp.dot(
            head_out, proj_ref[:, begin : begin + chunk], preferred_element_type=jnp.float32
        ).astype(out_ref.dtype)


def project(latents, value_up, out_proj):
    heads, latent, width = value_up.shape
    rows = latents[0].shape[0] // heads
    model = out_proj.shape[1]
    vmem = pl.BlockSpec(memory_space=pltpu.VMEM)
    return pl.pallas_call(
        project_kernel,
        in_specs=[vmem] * (2 + len(latents)),
        out_specs=vmem,
        out_shape=pltpu.VMEM((len(latents) * rows, model), jnp.bfloat16),
        compiler_params=pltpu.CompilerParams(vmem_limit_bytes=16 * MIB),
        cost_estimate=pl.CostEstimate(
            flops=2 * len(latents) * rows * out_proj.size,
            bytes_accessed=2 * (value_up.size + out_proj.size),
            transcendentals=0,
        ),
        name="project",
    )(value_up, out_proj, *latents)


def stage_kernel(count, after_ref, *refs):
    del after_ref
    sources, targets, (token, sems) = refs[:count], refs[count : 2 * count], refs[2 * count :]
    copies = [
        pltpu.make_async_copy(source, target, sems.at[number])
        for number, (source, target) in enumerate(zip(sources, targets))
    ]
    for copy in copies:
        copy.start()
    token[...] = jnp.zeros_like(token)
    for copy in copies:
        copy.wait()


def stage(after, values):
    anywhere = pl.BlockSpec(memory_space=pl.ANY)
    *staged, token = pl.pallas_call(
        functools.partial(stage_kernel, len(values)),
        in_specs=[anywhere] * (1 + len(values)),
        out_specs=[pl.BlockSpec(memory_space=pltpu.VMEM)] * (1 + len(values)),
        out_shape=[pltpu.VMEM(value.shape, value.dtype) for value in values]
        + [jax.ShapeDtypeStruct((8, LANES), jnp.float32)],
        scratch_shapes=[pltpu.SemaphoreType.DMA((len(values),))],
        compiler_params=pltpu.CompilerParams(vmem_limit_bytes=16 * MIB),
        cost_estimate=pl.CostEstimate(
            flops=0,
            bytes_accessed=2 * sum(value.size * value.dtype.itemsize for value in values),
            transcendentals=0,
        ),
        name="stage",
    )(after, *[in_hbm(value) for value in values])
    return staged, token


def lots_of(units):
    return [(begin, min(256, units - begin)) for begin in range(0, units, 256)]


def activate(rows, gate, up):
    gate_values = lax.dot_general(rows, gate, NT, preferred_element_type=jnp.float32)
    up_values = lax.dot_general(rows, up, NT, preferred_element_type=jnp.float32)
    return (gate_values / (1.0 + jnp.exp(-gate_values)) * up_values).astype(jnp.bfloat16)


def expert_kernel(blocks, slot_ref, after_ref, gate_ref, up_ref, down_ref, *refs):
    del after_ref
    inputs, outs, (rows, act) = refs[:blocks], refs[blocks:-2], refs[-2:]
    units, model = gate_ref.shape
    columns = 512
    slot = slot_ref[0]
    weights, at = [], 0
    for ref in inputs:
        rows[at : at + ref.shape[0], :] = ref[:, :model]
        at += ref.shape[0]
        tail = ref[:, model:].astype(jnp.float32)
        lane = lax.broadcasted_iota(jnp.int32, tail.shape, 1)
        mine = (lane == slot) | (lane == slot + tail.shape[1] // 2)
        weights.append(jnp.sum(jnp.where(mine, tail, 0.0), axis=1, keepdims=True))
    weight = jnp.concatenate(weights, axis=0)
    for begin, size in lots_of(units):
        lot = pl.ds(begin, size)
        act[:, begin : begin + size] = activate(rows[...], gate_ref[lot, :], up_ref[lot, :])
    for begin in range(0, model, columns):
        terms = weight * jnp.dot(
            act[...], down_ref[:, begin : begin + columns], preferred_element_type=jnp.float32
        )
        at = 0
        for out in outs:
            out[:, begin : begin + columns] = terms[at : at + out.shape[0]].astype(out.dtype)
            at += out.shape[0]


def run_experts(slot, after, gate, up, down, inputs, sizes):
    units, model = gate.shape
    total = sum(block.shape[0] for block in inputs)
    vmem = pl.BlockSpec(memory_space=pltpu.VMEM)
    return pl.pallas_call(
        functools.partial(expert_kernel, len(inputs)),
        in_specs=[pl.BlockSpec(memory_space=pltpu.SMEM), pl.BlockSpec(memory_space=pl.ANY)]
        + [vmem] * (3 + len(inputs)),
        out_specs=[vmem] * len(sizes),
        out_shape=[pltpu.VMEM((size, model), jnp.bfloat16) for size in sizes],
        scratch_shapes=[
            pltpu.VMEM((total, model), jnp.bfloat16),
            pltpu.VMEM((total, units), jnp.bfloat16),
        ],
        compiler_params=pltpu.CompilerParams(vmem_limit_bytes=28 * MIB),
        cost_estimate=pl.CostEstimate(flops=1, bytes_accessed=1, transcendentals=0),
        name="experts",
    )(slot, after, gate, up, down, *inputs)


def all_in_vmem(kernel, name, inputs, shapes):
    vmem = pl.BlockSpec(memory_space=pltpu.VMEM)
    return pl.pallas_call(
        kernel,
        in_specs=[vmem] * len(inputs),
        out_specs=[vmem] * len(shapes),
        out_shape=[pltpu.VMEM(shape, kind) for shape, kind in shapes],
        compiler_params=pltpu.CompilerParams(vmem_limit_bytes=8 * MIB),
        name=name,
    )(*inputs)


def add_kernel(crossed_ref, *refs):
    at = 0
    for mine, out in zip(refs[: len(refs) // 2], refs[len(refs) // 2 :]):
        other = crossed_ref[at : at + mine.shape[0], :]
        out[...] = (mine[...].astype(jnp.float32) + other.astype(jnp.float32)).astype(out.dtype)
        at += mine.shape[0]


def settle_kernel(mine_ref, crossed_ref, near, line, distant):
    total = mine_ref[...].astype(jnp.float32) + crossed_ref[...].astype(jnp.float32)
    rows = near.shape[0]
    near[...] = total[:rows]
    line[...] = total[rows : 2 * rows].astype(line.dtype)
    distant[...] = total[2 * rows :]


def merge_near_kernel(near_ref, line_ref, pair_ref, away_terms, own_terms, away, mixed):
    own = mixed.shape[0]
    total = near_ref[...] + line_ref[...].astype(jnp.float32)
    away[...] = (total[:own] + away_terms[...]).astype(away.dtype)
    mixed[...] = total[own:] + own_terms[...] + pair_ref[own:, :].astype(jnp.float32)


def merge_far_kernel(distant_ref, *refs):
    arrived, outs = refs[:3], refs[3:]
    total = distant_ref[...]
    for ref in arrived:
        total = total + ref[...].astype(jnp.float32)
    own = outs[0].shape[0]
    for number, out in enumerate(outs):
        out[...] = total[number * own : (number + 1) * own].astype(out.dtype)


def shared_kernel(gate_hbm, up_hbm, down_hbm, after_ref, rows_ref, *refs):
    del after_ref
    outs, (gate, up, down, act, sems) = refs[:-5], refs[-5:]
    rows = outs[0].shape[0]
    units, model = gate.shape
    lots, columns = lots_of(units), 1024
    copies = []
    for number, (begin, size) in enumerate(lots):
        for kind, (source, target) in enumerate(((gate_hbm, gate), (up_hbm, up))):
            lot = pl.ds(begin, size)
            copies.append(
                pltpu.make_async_copy(source.at[lot], target.at[lot], sems.at[kind, number])
            )
    copies.append(pltpu.make_async_copy(down_hbm, down, sems.at[2, 0]))
    for copy in copies:
        copy.start()
    for number, (begin, size) in enumerate(lots):
        copies[2 * number].wait()
        copies[2 * number + 1].wait()
        lot = pl.ds(begin, size)
        act[:, begin : begin + size] = activate(rows_ref[...], gate[lot, :], up[lot, :])
    copies[-1].wait()
    for begin in range(0, model, columns):
        terms = jnp.dot(
            act[...], down[:, begin : begin + columns], preferred_element_type=jnp.float32
        )
        for number, out in enumerate(outs):
            out[:, begin : begin + columns] = terms[number * rows : (number + 1) * rows]


def run_shared(after, rows, parts, gate, up, down):
    units, model = gate.shape
    vmem = pl.BlockSpec(memory_space=pltpu.VMEM)
    anywhere = pl.BlockSpec(memory_space=pl.ANY)
    return pl.pallas_call(
        shared_kernel,
        in_specs=[anywhere] * 4 + [vmem],
        out_specs=[vmem] * parts,
        out_shape=[pltpu.VMEM((rows.shape[0] // parts, model), jnp.float32)] * parts,
        scratch_shapes=[
            pltpu.VMEM(gate.shape, jnp.bfloat16),
            pltpu.VMEM(up.shape, jnp.bfloat16),
            pltpu.VMEM(down.shape, jnp.bfloat16),
            pltpu.VMEM((rows.shape[0], units), jnp.bfloat16),
            pltpu.SemaphoreType.DMA((3, len(lots_of(units)))),
        ],
        compiler_params=pltpu.CompilerParams(vmem_limit_bytes=24 * MIB),
        cost_estimate=pl.CostEstimate(
            flops=6 * rows.shape[0] * units * model,
            bytes_accessed=12 * units * model,
            transcendentals=rows.shape[0] * units,
        ),
        name="shared",
    )(*[in_hbm(value) for value in (gate, up, down)], after, rows)


def exchanges(groups, replicas):
    lines, depth = replicas, groups // (2 * replicas)

    def moves(dz=0, dy=0, dc=0, dx=0):
        pairs = []
        for group in range(groups):
            z, y, core = group // (2 * lines), group // 2 % lines, group % 2
            other = ((z + dz) % depth * lines + (y ^ dy)) * 2 + (core ^ dc)
            for rep in range(replicas):
                pairs.append((group * replicas + rep, other * replicas + (rep ^ dx)))
        return pairs

    return lambda value, **by: lax.ppermute(value, AXES, moves(**by))


def route_columns(routes, route_weight, placement):
    experts = placement.shape[0]
    ids = jnp.arange(experts, dtype=jnp.int32)
    slots = jnp.sum(jnp.where(routes[:, :, None] == ids, placement, 0), axis=2)
    table = jnp.sum(jnp.where(slots[:, :, None] == ids, route_weight[:, :, None], 0.0), axis=1)
    half = -(-experts // 64) * 64
    table = jnp.pad(table, ((0, 0), (0, half - experts)))
    high = table.astype(jnp.bfloat16)
    low = (table - high.astype(jnp.float32)).astype(jnp.bfloat16)
    return jnp.concatenate([high, low], axis=1)


def enter(attended, residual):
    attended = attended.astype(jnp.bfloat16).astype(jnp.float32)
    return (residual.astype(jnp.float32) + attended).astype(jnp.bfloat16)


def exchange_experts(swap, pair, columns, slot, weights, shared):
    own, model = pair.shape[0] // 2, pair.shape[1]
    directions = (dict(dx=1), dict(dy=1), dict(dx=1, dy=1))
    rows = jnp.concatenate([pair, columns], axis=1)
    line = [swap(rows[own:], dz=step) for step in (3, 2, 1)][::-1]
    across = swap(rows, dy=1)
    distant = jnp.concatenate(line, axis=0)
    distant, slot = lax.optimization_barrier((distant, slot))
    planes = [swap(distant, **by) for by in directions]
    early = [rows, across, distant]
    depth, width = sum(value.shape[0] for value in early), distant.shape[0]
    weights, token = stage(distant, weights)
    early += [swap(value, dc=1) for value in early]
    first = list(run_experts(slot, token, *weights, early, [depth, depth]))
    *planes, first[0], first[1] = lax.optimization_barrier((*planes, first[0], first[1]))
    others = [swap(plane, dc=1) for plane in planes]
    last = run_experts(slot, token, *weights, [*planes, *others], [width] * 3 + [3 * width])
    near, back, distant_sum = all_in_vmem(
        settle_kernel,
        "settle",
        [first[0], swap(first[1], dc=1)],
        [
            ((2 * own, model), jnp.float32),
            ((2 * own, model), jnp.bfloat16),
            ((width, model), jnp.float32),
        ],
    )
    crossed, back = lax.optimization_barrier((last[3], swap(back, dy=1)))
    sums = all_in_vmem(
        add_kernel,
        "add",
        [swap(crossed, dc=1), *last[:3]],
        [((width, model), jnp.bfloat16)] * 3,
    )
    returned = [swap(value, **by) for value, by in zip(sums, directions)]
    away_terms, own_terms = run_shared(sums[0], pair, 2, *shared)
    away, mixed = all_in_vmem(
        merge_near_kernel,
        "merge_near",
        [near, back, pair, away_terms, own_terms],
        [((own, model), jnp.bfloat16), ((own, model), jnp.float32)],
    )
    pieces = all_in_vmem(
        merge_far_kernel,
        "merge_far",
        [distant_sum, *returned],
        [((own, model), jnp.bfloat16)] * 3,
    )
    pieces = [swap(piece, dz=-step) for step, piece in zip((1, 2, 3), pieces)]
    return mixed, [*pieces, swap(away, dx=1)]


def finish_kernel(mixed_ref, gain_ref, *refs):
    pieces, out = refs[:-1], refs[-1]
    mixed = mixed_ref[...]
    for piece in pieces:
        mixed = mixed + piece[...].astype(jnp.float32)
    inverse = lax.rsqrt(jnp.mean(mixed * mixed, axis=1, keepdims=True) + EPSILON)
    out[...] = (mixed * inverse * gain_ref[...]).astype(out.dtype)


def finish(mixed, norm_gain, pieces=()):
    vmem = pl.BlockSpec(memory_space=pltpu.VMEM)
    return pl.pallas_call(
        finish_kernel,
        in_specs=[vmem] * (2 + len(pieces)),
        out_specs=vmem,
        out_shape=jax.ShapeDtypeStruct(mixed.shape, jnp.bfloat16),
        compiler_params=pltpu.CompilerParams(vmem_limit_bytes=8 * MIB),
        name="finish",
    )(mixed, norm_gain.reshape(1, -1), *pieces)


def per_device(
    residual,
    query_latent,
    query_rope,
    cache_latent,
    cache_rope,
    page_table,
    lengths,
    value_up,
    out_proj,
    routes,
    route_weight,
    placement,
    expert_gate,
    expert_up,
    expert_down,
    shared_gate,
    shared_up,
    shared_down,
    norm_gain,
):
    replicas = lax.axis_size("rep")
    groups = lax.axis_size("ep")
    rep = lax.axis_index("rep")
    slot = lax.axis_index("ep").reshape(1).astype(jnp.int32)
    own = page_table.shape[0]
    heads = value_up.shape[0]
    own_rows = lambda value: lax.dynamic_slice_in_dim(value, rep * own, own, 0)
    caches = (query_latent, query_rope, cache_latent, cache_rope, page_table, lengths)
    gate = expert_gate[0].T
    up = expert_up[0].T
    down = expert_down[0]
    shared = (shared_gate.T, shared_up.T, shared_down)
    if replicas == 2 and groups == 16:
        swap = exchanges(groups, replicas)
        own_last = lambda value: lax.dynamic_slice_in_dim(
            jnp.concatenate([value, value], axis=0), (1 - rep) * own, 2 * own, 0
        )
        away, prepared = attend(1 - rep, heads, *caches)
        arrived = swap(away, dx=1)
        kept, value_up, out_proj = attend_more(
            rep, heads, prepared, query_latent, query_rope, (value_up, out_proj)
        )
        terms = project([arrived, kept], value_up, out_proj)
        terms, routing = lax.optimization_barrier((terms, (routes, route_weight, residual)))
        routes, route_weight, residual = routing
        back = swap(terms, dx=1)
        columns = own_last(route_columns(routes, route_weight, placement))
        residual = own_last(residual)
        back = jnp.concatenate([back[own:], back[:own]], axis=0)
        pair = enter(terms.astype(jnp.float32) + back.astype(jnp.float32), residual)
        mixed, pieces = exchange_experts(swap, pair, columns, slot, (gate, up, down), shared)
        return finish(mixed, norm_gain, pieces)

    latents, _ = attend(jnp.int32(0), heads * replicas, *caches)
    latents = lax.all_to_all(latents, "rep", 0, 0, tiled=True)
    latents = latents.reshape(replicas, -1, latents.shape[1])
    terms = project([latents[i] for i in range(replicas)], value_up, out_proj)
    attended = lax.psum_scatter(terms, "rep", scatter_dimension=0, tiled=True)
    hidden = enter(attended, own_rows(residual))
    model = hidden.shape[1]
    columns = route_columns(own_rows(routes), own_rows(route_weight), placement)
    block = jnp.concatenate([hidden, columns], axis=1)
    every = lax.all_gather(block, AXES, axis=0, tiled=True)
    lot = min(512, every.shape[0])
    terms = [
        run_experts(slot, slot, gate, up, down, [every[at : at + lot]], [lot])[0]
        for at in range(0, every.shape[0], lot)
    ]
    mine = lax.dynamic_slice_in_dim(every, slot[0] * replicas * own, replicas * own, 0)[:, :model]
    own_terms = run_shared(mine, mine, 1, *shared)[0].astype(jnp.bfloat16)
    total = lax.psum_scatter(
        jnp.concatenate(terms, axis=0), AXES, scatter_dimension=0, tiled=True
    ).astype(jnp.float32)
    total = total + lax.psum_scatter(
        own_terms, "rep", scatter_dimension=0, tiled=True
    ).astype(jnp.float32)
    return finish(hidden.astype(jnp.float32) + total, norm_gain)


def solution(mesh):
    in_specs = (
        P("ep", None),
        P(("ep", "rep"), None),
        P(("ep", "rep"), None),
        P(("ep", "rep"), None, None),
        P(("ep", "rep"), None),
        P(("ep", "rep"), None),
        P(("ep", "rep")),
        P("rep", None, None),
        P("rep", None),
        P("ep", None),
        P("ep", None),
        P(),
        P("ep", None, "rep"),
        P("ep", None, "rep"),
        P("ep", "rep", None),
        P(None, "rep"),
        P(None, "rep"),
        P("rep", None),
        P(),
    )
    out_specs = P(("ep", "rep"), None)
    return jax.shard_map(
        per_device, mesh=mesh, in_specs=in_specs, out_specs=out_specs, check_vma=False
    )
```

```python
import functools
import math

import jax
import jax.numpy as jnp
from jax import lax
from jax.experimental import pallas as pl
from jax.experimental.pallas import tpu as pltpu
from jax.sharding import PartitionSpec as P

ROPE = 64
VHEAD = 128
LANES = 128
EPSILON = 1e-06
AXES = ("ep", "rep")
MIB = 1024 * 1024
NT = (((1,), (1,)), ((), ()))


def in_hbm(value):
    return pltpu.with_memory_space_constraint(value, pltpu.HBM)


def attend_heads(query_ref, rot_ref, key_lat, key_rot, count, out_ref, before_latent, before_keys):
    rows, keys = count.shape
    latent = key_lat.shape[1]
    heads = out_ref.shape[0] // rows
    low = lax.broadcasted_iota(jnp.int32, (rows, LANES), 1) < ROPE
    rot_parts = []
    for head in range(heads):
        pair = rot_ref[:, head // 2 * LANES : (head // 2 + 1) * LANES].astype(jnp.float32)
        if head % 2:
            pair = pltpu.roll(pair, ROPE, 1)
        rot_parts.append(jnp.where(low, pair, 0.0).astype(jnp.bfloat16))
    rot = jnp.concatenate(rot_parts, axis=0)
    scores = lax.dot_general(rot, key_rot[...], NT, preferred_element_type=jnp.float32)
    before_latent()
    query = jnp.concatenate(
        [query_ref[:, head * latent : (head + 1) * latent] for head in range(heads)], axis=0
    )
    before_keys()
    scores = (
        lax.dot_general(query, key_lat[...], NT, preferred_element_type=jnp.float32) + scores
    ) * (1.0 / math.sqrt(VHEAD + ROPE))
    scores = scores.reshape(heads, rows, keys)
    counts = count[...][None]
    masked = jnp.where(counts > 0.0, scores, -jnp.inf)
    peak = jnp.max(masked, axis=2, keepdims=True)
    expons = jnp.exp(masked - peak) * counts
    probs = (expons / jnp.sum(expons, axis=2, keepdims=True)).astype(jnp.bfloat16)
    out_ref[...] = jnp.dot(
        probs.reshape(heads * rows, keys), key_lat[...], preferred_element_type=jnp.float32
    ).astype(jnp.bfloat16)


def head_columns(ref, head_block, width):
    return ref.at[:, pl.ds(pl.multiple_of(head_block * width, LANES), width)]


def attend_kernel(
    block_ref,
    lengths_hbm,
    table_hbm,
    query_hbm,
    rot_hbm,
    pages_hbm,
    rope_hbm,
    out_ref,
    key_lat,
    key_rot,
    count,
    lengths_ref,
    table_ref,
    query_ref,
    rot_ref,
    rope_ref,
    keys_rope,
    sems,
):
    rows, span = table_ref.shape
    pages, page_len, latent = pages_hbm.shape
    keys = pages * page_len
    copies = [
        pltpu.make_async_copy(source, target, sems.at[number])
        for number, (source, target) in enumerate(
            (
                (rope_hbm, rope_ref),
                (table_hbm, table_ref),
                (lengths_hbm, lengths_ref),
                (head_columns(rot_hbm, block_ref[0], rot_ref.shape[1]), rot_ref),
                (head_columns(query_hbm, block_ref[0], query_ref.shape[1]), query_ref),
                (pages_hbm, key_lat.reshape(pages, page_len, latent)),
            )
        )
    ]
    for copy in copies:
        copy.start()
    copies[0].wait()
    for pair in range(page_len // 2):
        both = rope_ref[:, pair * LANES : (pair + 1) * LANES].astype(jnp.float32)
        keys_rope[pl.ds(2 * pair, pages, stride=page_len), :] = both
        keys_rope[pl.ds(2 * pair + 1, pages, stride=page_len), :] = pltpu.roll(both, ROPE, 1)
    key_rot[...] = keys_rope[...].astype(jnp.bfloat16)
    copies[1].wait()
    copies[2].wait()
    row_ids = lax.broadcasted_iota(jnp.int32, (rows, LANES), 0)
    lengths = jnp.zeros((rows, LANES), jnp.int32)
    for row in range(rows):
        lengths = jnp.where(row_ids == row, lengths_ref[row], lengths)
    lengths = lengths[:, :1]
    key_ids = lax.broadcasted_iota(jnp.int32, (rows, keys), 1)
    page_of, slot_of = key_ids // page_len, key_ids % page_len
    total = jnp.zeros((rows, keys), jnp.float32)
    for step in range(span):
        live = (table_ref[:, step : step + 1] == page_of) & (slot_of + step * page_len < lengths)
        total = total + jnp.where(live, 1.0, 0.0)
    count[...] = total
    copies[3].wait()
    attend_heads(
        query_ref, rot_ref, key_lat, key_rot, count, out_ref, copies[4].wait, copies[5].wait
    )


def attend(block, heads, query_latent, query_rope, cache_latent, cache_rope, page_table, lengths):
    rows = page_table.shape[0]
    pages, page_len, latent = cache_latent.shape
    keys = pages * page_len
    operands = (lengths, page_table, query_latent, query_rope, cache_latent, cache_rope)
    out, *prepared = pl.pallas_call(
        attend_kernel,
        in_specs=[pl.BlockSpec(memory_space=pltpu.SMEM)]
        + [pl.BlockSpec(memory_space=pl.ANY)] * len(operands),
        out_specs=[pl.BlockSpec(memory_space=pltpu.VMEM)] * 4,
        out_shape=[
            pltpu.VMEM((heads * rows, latent), jnp.bfloat16),
            pltpu.VMEM((keys, latent), jnp.bfloat16),
            pltpu.VMEM((keys, LANES), jnp.bfloat16),
            pltpu.VMEM((rows, keys), jnp.float32),
        ],
        scratch_shapes=[
            pltpu.SMEM(lengths.shape, jnp.int32),
            pltpu.VMEM(page_table.shape, jnp.int32),
            pltpu.VMEM((rows, heads * latent), jnp.bfloat16),
            pltpu.VMEM((rows, heads * ROPE), jnp.bfloat16),
            pltpu.VMEM(cache_rope.shape, jnp.bfloat16),
            pltpu.VMEM((keys, LANES), jnp.float32),
            pltpu.SemaphoreType.DMA((len(operands),)),
        ],
        compiler_params=pltpu.CompilerParams(vmem_limit_bytes=16 * MIB),
        cost_estimate=pl.CostEstimate(
            flops=4 * heads * rows * keys * latent,
            bytes_accessed=4 * MIB,
            transcendentals=heads * rows * keys,
        ),
        name="attend",
    )(block.reshape(1).astype(jnp.int32), *[in_hbm(value) for value in operands])
    return out, prepared


def attend_more_kernel(
    staged, block_ref, key_lat, key_rot, count, query_hbm, rot_hbm, *refs
):
    sources, (out_ref, *targets) = refs[:staged], refs[staged : 2 * staged + 1]
    query_ref, rot_ref, sems = refs[2 * staged + 1 :]
    copies = [
        pltpu.make_async_copy(source, target, sems.at[number])
        for number, (source, target) in enumerate(
            (
                (head_columns(rot_hbm, block_ref[0], rot_ref.shape[1]), rot_ref),
                (head_columns(query_hbm, block_ref[0], query_ref.shape[1]), query_ref),
                *zip(sources, targets),
            )
        )
    ]
    for copy in copies:
        copy.start()
    copies[0].wait()
    attend_heads(
        query_ref, rot_ref, key_lat, key_rot, count, out_ref, copies[1].wait, lambda: None
    )
    for copy in copies[2:]:
        copy.wait()


def attend_more(block, heads, prepared, query_latent, query_rope, values):
    key_lat, key_rot, count = prepared
    rows, keys = count.shape
    latent = key_lat.shape[1]
    vmem = pl.BlockSpec(memory_space=pltpu.VMEM)
    anywhere = pl.BlockSpec(memory_space=pl.ANY)
    return pl.pallas_call(
        functools.partial(attend_more_kernel, len(values)),
        in_specs=[pl.BlockSpec(memory_space=pltpu.SMEM)] + [vmem] * 3 + [anywhere] * (2 + len(values)),
        out_specs=[vmem] * (1 + len(values)),
        out_shape=[pltpu.VMEM((heads * rows, latent), jnp.bfloat16)]
        + [pltpu.VMEM(value.shape, value.dtype) for value in values],
        scratch_shapes=[
            pltpu.VMEM((rows, heads * latent), jnp.bfloat16),
            pltpu.VMEM((rows, heads * ROPE), jnp.bfloat16),
            pltpu.SemaphoreType.DMA((2 + len(values),)),
        ],
        compiler_params=pltpu.CompilerParams(vmem_limit_bytes=16 * MIB),
        cost_estimate=pl.CostEstimate(
            flops=4 * heads * rows * keys * latent,
            bytes_accessed=8 * MIB,
            transcendentals=heads * rows * keys,
        ),
        name="attend_more",
    )(
        block.reshape(1).astype(jnp.int32),
        *prepared,
        *[in_hbm(value) for value in (query_latent, query_rope, *values)],
    )


def project_kernel(value_ref, proj_ref, *refs):
    latents, out_ref = refs[:-1], refs[-1]
    heads, latent, width = value_ref.shape
    rows = latents[0].shape[0] // heads
    outs = []
    for head in range(heads):
        both = jnp.concatenate(
            [ref[head * rows : (head + 1) * rows, :] for ref in latents], axis=0
        )
        outs.append(
            jnp.dot(both, value_ref[head], preferred_element_type=jnp.float32).astype(jnp.bfloat16)
        )
    head_out = jnp.concatenate(outs, axis=1)
    chunk = 512
    for begin in range(0, proj_ref.shape[1], chunk):
        out_ref[:, begin : begin + chunk] = jnp.dot(
            head_out, proj_ref[:, begin : begin + chunk], preferred_element_type=jnp.float32
        ).astype(out_ref.dtype)


def project(latents, value_up, out_proj):
    heads, latent, width = value_up.shape
    rows = latents[0].shape[0] // heads
    model = out_proj.shape[1]
    vmem = pl.BlockSpec(memory_space=pltpu.VMEM)
    return pl.pallas_call(
        project_kernel,
        in_specs=[vmem] * (2 + len(latents)),
        out_specs=vmem,
        out_shape=pltpu.VMEM((len(latents) * rows, model), jnp.bfloat16),
        compiler_params=pltpu.CompilerParams(vmem_limit_bytes=16 * MIB),
        cost_estimate=pl.CostEstimate(
            flops=2 * len(latents) * rows * out_proj.size,
            bytes_accessed=2 * (value_up.size + out_proj.size),
            transcendentals=0,
        ),
        name="project",
    )(value_up, out_proj, *latents)


def stage_kernel(count, after_ref, *refs):
    del after_ref
    sources, targets, (token, sems) = refs[:count], refs[count : 2 * count], refs[2 * count :]
    copies = [
        pltpu.make_async_copy(source, target, sems.at[number])
        for number, (source, target) in enumerate(zip(sources, targets))
    ]
    for copy in copies:
        copy.start()
    token[...] = jnp.zeros_like(token)
    for copy in copies:
        copy.wait()


def stage(after, values):
    anywhere = pl.BlockSpec(memory_space=pl.ANY)
    *staged, token = pl.pallas_call(
        functools.partial(stage_kernel, len(values)),
        in_specs=[anywhere] * (1 + len(values)),
        out_specs=[pl.BlockSpec(memory_space=pltpu.VMEM)] * (1 + len(values)),
        out_shape=[pltpu.VMEM(value.shape, value.dtype) for value in values]
        + [jax.ShapeDtypeStruct((8, LANES), jnp.float32)],
        scratch_shapes=[pltpu.SemaphoreType.DMA((len(values),))],
        compiler_params=pltpu.CompilerParams(vmem_limit_bytes=16 * MIB),
        cost_estimate=pl.CostEstimate(
            flops=0,
            bytes_accessed=2 * sum(value.size * value.dtype.itemsize for value in values),
            transcendentals=0,
        ),
        name="stage",
    )(after, *[in_hbm(value) for value in values])
    return staged, token


def lots_of(units):
    return [(begin, min(256, units - begin)) for begin in range(0, units, 256)]


def activate(rows, gate, up):
    gate_values = lax.dot_general(rows, gate, NT, preferred_element_type=jnp.float32)
    up_values = lax.dot_general(rows, up, NT, preferred_element_type=jnp.float32)
    return (gate_values / (1.0 + jnp.exp(-gate_values)) * up_values).astype(jnp.bfloat16)


def expert_kernel(blocks, slot_ref, after_ref, gate_ref, up_ref, down_ref, *refs):
    del after_ref
    inputs, outs, (rows, act) = refs[:blocks], refs[blocks:-2], refs[-2:]
    units, model = gate_ref.shape
    columns = 512
    slot = slot_ref[0]
    tails = min(ref.shape[1] for ref in inputs) - model
    weights, at = [], 0
    for ref in inputs:
        rows[at : at + ref.shape[0], :] = ref[:, :model]
        at += ref.shape[0]
        tail = ref[:, model : model + tails].astype(jnp.float32)
        lane = lax.broadcasted_iota(jnp.int32, tail.shape, 1)
        mine = (lane == slot) | (lane == slot + tail.shape[1] // 2)
        weights.append(jnp.sum(jnp.where(mine, tail, 0.0), axis=1, keepdims=True))
    weight = jnp.concatenate(weights, axis=0)
    for begin, size in lots_of(units):
        lot = pl.ds(begin, size)
        act[:, begin : begin + size] = activate(rows[...], gate_ref[lot, :], up_ref[lot, :])
    for begin in range(0, model, columns):
        terms = weight * jnp.dot(
            act[...], down_ref[:, begin : begin + columns], preferred_element_type=jnp.float32
        )
        at = 0
        for out in outs:
            out[:, begin : begin + columns] = terms[at : at + out.shape[0]].astype(out.dtype)
            at += out.shape[0]


def run_experts(slot, after, gate, up, down, inputs, sizes):
    units, model = gate.shape
    total = sum(block.shape[0] for block in inputs)
    vmem = pl.BlockSpec(memory_space=pltpu.VMEM)
    return pl.pallas_call(
        functools.partial(expert_kernel, len(inputs)),
        in_specs=[pl.BlockSpec(memory_space=pltpu.SMEM), pl.BlockSpec(memory_space=pl.ANY)]
        + [vmem] * (3 + len(inputs)),
        out_specs=[vmem] * len(sizes),
        out_shape=[pltpu.VMEM((size, model), jnp.bfloat16) for size in sizes],
        scratch_shapes=[
            pltpu.VMEM((total, model), jnp.bfloat16),
            pltpu.VMEM((total, units), jnp.bfloat16),
        ],
        compiler_params=pltpu.CompilerParams(vmem_limit_bytes=28 * MIB),
        cost_estimate=pl.CostEstimate(flops=1, bytes_accessed=1, transcendentals=0),
        name="experts",
    )(slot, after, gate, up, down, *inputs)


def all_in_vmem(kernel, name, inputs, shapes):
    vmem = pl.BlockSpec(memory_space=pltpu.VMEM)
    return pl.pallas_call(
        kernel,
        in_specs=[vmem] * len(inputs),
        out_specs=[vmem] * len(shapes),
        out_shape=[pltpu.VMEM(shape, kind) for shape, kind in shapes],
        compiler_params=pltpu.CompilerParams(vmem_limit_bytes=8 * MIB),
        name=name,
    )(*inputs)


def add_kernel(crossed_ref, *refs):
    at = 0
    for mine, out in zip(refs[: len(refs) // 2], refs[len(refs) // 2 :]):
        other = crossed_ref[at : at + mine.shape[0], :]
        total = mine[...].astype(jnp.float32) + other.astype(jnp.float32)
        out[:, : total.shape[1]] = total.astype(out.dtype)
        if out.shape[1] > total.shape[1]:
            out[:, total.shape[1] :] = jnp.zeros((out.shape[0], LANES), out.dtype)
        at += mine.shape[0]


def settle_kernel(mine_ref, crossed_ref, near, line, distant):
    total = mine_ref[...].astype(jnp.float32) + crossed_ref[...].astype(jnp.float32)
    rows = near.shape[0]
    near[...] = total[:rows]
    line[...] = total[rows : 2 * rows].astype(line.dtype)
    distant[...] = total[2 * rows :]


def merge_near_kernel(near_ref, line_ref, pair_ref, away_terms, own_terms, away, mixed):
    own = mixed.shape[0]
    total = near_ref[...] + line_ref[...].astype(jnp.float32)
    away[...] = (total[:own] + away_terms[...]).astype(away.dtype)
    mixed[...] = total[own:] + own_terms[...] + pair_ref[own:, :].astype(jnp.float32)


def merge_far_kernel(distant_ref, *refs):
    arrived, outs = refs[:3], refs[3:]
    total = distant_ref[...]
    for ref in arrived:
        total = total + ref[:, : total.shape[1]].astype(jnp.float32)
    own = outs[0].shape[0]
    for number, out in enumerate(outs):
        out[...] = total[number * own : (number + 1) * own].astype(out.dtype)


def shared_kernel(gate_hbm, up_hbm, down_hbm, after_ref, rows_ref, *refs):
    del after_ref
    outs, (gate, up, down, act, sems) = refs[:-5], refs[-5:]
    rows = outs[0].shape[0]
    units, model = gate.shape
    lots, columns = lots_of(units), 1024
    copies = []
    for number, (begin, size) in enumerate(lots):
        for kind, (source, target) in enumerate(((gate_hbm, gate), (up_hbm, up))):
            lot = pl.ds(begin, size)
            copies.append(
                pltpu.make_async_copy(source.at[lot], target.at[lot], sems.at[kind, number])
            )
    copies.append(pltpu.make_async_copy(down_hbm, down, sems.at[2, 0]))
    for copy in copies:
        copy.start()
    for number, (begin, size) in enumerate(lots):
        copies[2 * number].wait()
        copies[2 * number + 1].wait()
        lot = pl.ds(begin, size)
        act[:, begin : begin + size] = activate(rows_ref[...], gate[lot, :], up[lot, :])
    copies[-1].wait()
    for begin in range(0, model, columns):
        terms = jnp.dot(
            act[...], down[:, begin : begin + columns], preferred_element_type=jnp.float32
        )
        for number, out in enumerate(outs):
            out[:, begin : begin + columns] = terms[number * rows : (number + 1) * rows]


def run_shared(after, rows, parts, gate, up, down):
    units, model = gate.shape
    vmem = pl.BlockSpec(memory_space=pltpu.VMEM)
    anywhere = pl.BlockSpec(memory_space=pl.ANY)
    return pl.pallas_call(
        shared_kernel,
        in_specs=[anywhere] * 4 + [vmem],
        out_specs=[vmem] * parts,
        out_shape=[pltpu.VMEM((rows.shape[0] // parts, model), jnp.float32)] * parts,
        scratch_shapes=[
            pltpu.VMEM(gate.shape, jnp.bfloat16),
            pltpu.VMEM(up.shape, jnp.bfloat16),
            pltpu.VMEM(down.shape, jnp.bfloat16),
            pltpu.VMEM((rows.shape[0], units), jnp.bfloat16),
            pltpu.SemaphoreType.DMA((3, len(lots_of(units)))),
        ],
        compiler_params=pltpu.CompilerParams(vmem_limit_bytes=24 * MIB),
        cost_estimate=pl.CostEstimate(
            flops=6 * rows.shape[0] * units * model,
            bytes_accessed=12 * units * model,
            transcendentals=rows.shape[0] * units,
        ),
        name="shared",
    )(*[in_hbm(value) for value in (gate, up, down)], after, rows)


def exchanges(groups, replicas):
    lines, depth = replicas, groups // (2 * replicas)

    def moves(dz=0, dy=0, dc=0, dx=0):
        pairs = []
        for group in range(groups):
            z, y, core = group // (2 * lines), group // 2 % lines, group % 2
            other = ((z + dz) % depth * lines + (y ^ dy)) * 2 + (core ^ dc)
            for rep in range(replicas):
                pairs.append((group * replicas + rep, other * replicas + (rep ^ dx)))
        return pairs

    return lambda value, **by: lax.ppermute(value, AXES, moves(**by))


def route_columns(routes, route_weight, placement):
    experts = placement.shape[0]
    ids = jnp.arange(experts, dtype=jnp.int32)
    slots = jnp.sum(jnp.where(routes[:, :, None] == ids, placement, 0), axis=2)
    table = jnp.sum(jnp.where(slots[:, :, None] == ids, route_weight[:, :, None], 0.0), axis=1)
    half = -(-experts // 64) * 64
    table = jnp.pad(table, ((0, 0), (0, half - experts)))
    high = table.astype(jnp.bfloat16)
    low = (table - high.astype(jnp.float32)).astype(jnp.bfloat16)
    return jnp.concatenate([high, low], axis=1)


def enter(attended, residual):
    attended = attended.astype(jnp.bfloat16).astype(jnp.float32)
    return (residual.astype(jnp.float32) + attended).astype(jnp.bfloat16)


def exchange_experts(swap, pair, columns, slot, weights, shared):
    own, model = pair.shape[0] // 2, pair.shape[1]
    directions = (dict(dx=1), dict(dy=1), dict(dx=1, dy=1))
    rows = jnp.concatenate([pair, columns], axis=1)
    line = [swap(rows[own:], dz=step) for step in (3, 2, 1)][::-1]
    across = swap(rows, dy=1)
    distant = jnp.concatenate(line, axis=0)
    wide = jnp.concatenate([distant, jnp.zeros((distant.shape[0], LANES), distant.dtype)], axis=1)
    distant, wide, slot = lax.optimization_barrier((distant, wide, slot))
    sent = (distant, distant, wide)
    planes = [swap(value, **by) for value, by in zip(sent, directions)]
    early = [rows, across, distant]
    depth, width = sum(value.shape[0] for value in early), distant.shape[0]
    weights, token = stage(distant, weights)
    early += [swap(value, dc=1) for value in early]
    first = list(run_experts(slot, token, *weights, early, [depth, depth]))
    *planes, first[0], first[1] = lax.optimization_barrier((*planes, first[0], first[1]))
    others = [swap(plane, dc=1) for plane in planes]
    last = run_experts(slot, token, *weights, [*planes, *others], [width] * 3 + [3 * width])
    near, back, distant_sum = all_in_vmem(
        settle_kernel,
        "settle",
        [first[0], swap(first[1], dc=1)],
        [
            ((2 * own, model), jnp.float32),
            ((2 * own, model), jnp.bfloat16),
            ((width, model), jnp.float32),
        ],
    )
    crossed, back = lax.optimization_barrier((last[3], swap(back, dy=1)))
    sums = all_in_vmem(
        add_kernel,
        "add",
        [swap(crossed, dc=1), *last[:3]],
        [((width, model + more), jnp.bfloat16) for more in (0, 0, 0)],
    )
    returned = [swap(value, **by) for value, by in zip(sums, directions)]
    away_terms, own_terms = run_shared(sums[0], pair, 2, *shared)
    away, mixed = all_in_vmem(
        merge_near_kernel,
        "merge_near",
        [near, back, pair, away_terms, own_terms],
        [((own, model), jnp.bfloat16), ((own, model), jnp.float32)],
    )
    pieces = all_in_vmem(
        merge_far_kernel,
        "merge_far",
        [distant_sum, *returned],
        [((own, model), jnp.bfloat16)] * 3,
    )
    pieces = [swap(piece, dz=-step) for step, piece in zip((1, 2, 3), pieces)]
    return mixed, [*pieces, swap(away, dx=1)]


def finish_kernel(mixed_ref, gain_ref, *refs):
    pieces, out = refs[:-1], refs[-1]
    mixed = mixed_ref[...]
    for piece in pieces:
        mixed = mixed + piece[...].astype(jnp.float32)
    inverse = lax.rsqrt(jnp.mean(mixed * mixed, axis=1, keepdims=True) + EPSILON)
    out[...] = (mixed * inverse * gain_ref[...]).astype(out.dtype)


def finish(mixed, norm_gain, pieces=()):
    vmem = pl.BlockSpec(memory_space=pltpu.VMEM)
    return pl.pallas_call(
        finish_kernel,
        in_specs=[vmem] * (2 + len(pieces)),
        out_specs=vmem,
        out_shape=jax.ShapeDtypeStruct(mixed.shape, jnp.bfloat16),
        compiler_params=pltpu.CompilerParams(vmem_limit_bytes=8 * MIB),
        name="finish",
    )(mixed, norm_gain.reshape(1, -1), *pieces)


def per_device(
    residual,
    query_latent,
    query_rope,
    cache_latent,
    cache_rope,
    page_table,
    lengths,
    value_up,
    out_proj,
    routes,
    route_weight,
    placement,
    expert_gate,
    expert_up,
    expert_down,
    shared_gate,
    shared_up,
    shared_down,
    norm_gain,
):
    replicas = lax.axis_size("rep")
    groups = lax.axis_size("ep")
    rep = lax.axis_index("rep")
    slot = lax.axis_index("ep").reshape(1).astype(jnp.int32)
    own = page_table.shape[0]
    heads = value_up.shape[0]
    own_rows = lambda value: lax.dynamic_slice_in_dim(value, rep * own, own, 0)
    caches = (query_latent, query_rope, cache_latent, cache_rope, page_table, lengths)
    gate = expert_gate[0].T
    up = expert_up[0].T
    down = expert_down[0]
    shared = (shared_gate.T, shared_up.T, shared_down)
    if replicas == 2 and groups == 16:
        swap = exchanges(groups, replicas)
        own_last = lambda value: lax.dynamic_slice_in_dim(
            jnp.concatenate([value, value], axis=0), (1 - rep) * own, 2 * own, 0
        )
        away, prepared = attend(1 - rep, heads, *caches)
        arrived = swap(away, dx=1)
        kept, value_up, out_proj = attend_more(
            rep, heads, prepared, query_latent, query_rope, (value_up, out_proj)
        )
        terms = project([arrived, kept], value_up, out_proj)
        terms, routing = lax.optimization_barrier((terms, (routes, route_weight, residual)))
        routes, route_weight, residual = routing
        back = swap(terms, dx=1)
        columns = own_last(route_columns(routes, route_weight, placement))
        residual = own_last(residual)
        back = jnp.concatenate([back[own:], back[:own]], axis=0)
        pair = enter(terms.astype(jnp.float32) + back.astype(jnp.float32), residual)
        mixed, pieces = exchange_experts(swap, pair, columns, slot, (gate, up, down), shared)
        return finish(mixed, norm_gain, pieces)

    latents, _ = attend(jnp.int32(0), heads * replicas, *caches)
    latents = lax.all_to_all(latents, "rep", 0, 0, tiled=True)
    latents = latents.reshape(replicas, -1, latents.shape[1])
    terms = project([latents[i] for i in range(replicas)], value_up, out_proj)
    attended = lax.psum_scatter(terms, "rep", scatter_dimension=0, tiled=True)
    hidden = enter(attended, own_rows(residual))
    model = hidden.shape[1]
    columns = route_columns(own_rows(routes), own_rows(route_weight), placement)
    block = jnp.concatenate([hidden, columns], axis=1)
    every = lax.all_gather(block, AXES, axis=0, tiled=True)
    lot = min(512, every.shape[0])
    terms = [
        run_experts(slot, slot, gate, up, down, [every[at : at + lot]], [lot])[0]
        for at in range(0, every.shape[0], lot)
    ]
    mine = lax.dynamic_slice_in_dim(every, slot[0] * replicas * own, replicas * own, 0)[:, :model]
    own_terms = run_shared(mine, mine, 1, *shared)[0].astype(jnp.bfloat16)
    total = lax.psum_scatter(
        jnp.concatenate(terms, axis=0), AXES, scatter_dimension=0, tiled=True
    ).astype(jnp.float32)
    total = total + lax.psum_scatter(
        own_terms, "rep", scatter_dimension=0, tiled=True
    ).astype(jnp.float32)
    return finish(hidden.astype(jnp.float32) + total, norm_gain)


def solution(mesh):
    in_specs = (
        P("ep", None),
        P(("ep", "rep"), None),
        P(("ep", "rep"), None),
        P(("ep", "rep"), None, None),
        P(("ep", "rep"), None),
        P(("ep", "rep"), None),
        P(("ep", "rep")),
        P("rep", None, None),
        P("rep", None),
        P("ep", None),
        P("ep", None),
        P(),
        P("ep", None, "rep"),
        P("ep", None, "rep"),
        P("ep", "rep", None),
        P(None, "rep"),
        P(None, "rep"),
        P("rep", None),
        P(),
    )
    out_specs = P(("ep", "rep"), None)
    return jax.shard_map(
        per_device, mesh=mesh, in_specs=in_specs, out_specs=out_specs, check_vma=False
    )
```

```python
import functools
import math

import jax
import jax.numpy as jnp
from jax import lax
from jax.experimental import pallas as pl
from jax.experimental.pallas import tpu as pltpu
from jax.sharding import PartitionSpec as P

ROPE = 64
VHEAD = 128
LANES = 128
EPSILON = 1e-06
AXES = ("ep", "rep")
MIB = 1024 * 1024
NT = (((1,), (1,)), ((), ()))


def in_hbm(value):
    return pltpu.with_memory_space_constraint(value, pltpu.HBM)


def attend_heads(query_ref, rot_ref, key_lat, key_rot, count, out_ref, before_latent, before_keys):
    rows, keys = count.shape
    latent = key_lat.shape[1]
    heads = out_ref.shape[0] // rows
    low = lax.broadcasted_iota(jnp.int32, (rows, LANES), 1) < ROPE
    rot_parts = []
    for head in range(heads):
        pair = rot_ref[:, head // 2 * LANES : (head // 2 + 1) * LANES].astype(jnp.float32)
        if head % 2:
            pair = pltpu.roll(pair, ROPE, 1)
        rot_parts.append(jnp.where(low, pair, 0.0).astype(jnp.bfloat16))
    rot = jnp.concatenate(rot_parts, axis=0)
    scores = lax.dot_general(rot, key_rot[...], NT, preferred_element_type=jnp.float32)
    before_latent()
    query = jnp.concatenate(
        [query_ref[:, head * latent : (head + 1) * latent] for head in range(heads)], axis=0
    )
    before_keys()
    scores = (
        lax.dot_general(query, key_lat[...], NT, preferred_element_type=jnp.float32) + scores
    ) * (1.0 / math.sqrt(VHEAD + ROPE))
    scores = scores.reshape(heads, rows, keys)
    counts = count[...][None]
    masked = jnp.where(counts > 0.0, scores, -jnp.inf)
    peak = jnp.max(masked, axis=2, keepdims=True)
    expons = jnp.exp(masked - peak) * counts
    probs = (expons / jnp.sum(expons, axis=2, keepdims=True)).astype(jnp.bfloat16)
    out_ref[...] = jnp.dot(
        probs.reshape(heads * rows, keys), key_lat[...], preferred_element_type=jnp.float32
    ).astype(jnp.bfloat16)


def head_columns(ref, head_block, width):
    return ref.at[:, pl.ds(pl.multiple_of(head_block * width, LANES), width)]


def attend_kernel(
    block_ref,
    lengths_hbm,
    table_hbm,
    query_hbm,
    rot_hbm,
    pages_hbm,
    rope_hbm,
    out_ref,
    key_lat,
    key_rot,
    count,
    lengths_ref,
    table_ref,
    query_ref,
    rot_ref,
    rope_ref,
    keys_rope,
    sems,
):
    rows, span = table_ref.shape
    pages, page_len, latent = pages_hbm.shape
    keys = pages * page_len
    copies = [
        pltpu.make_async_copy(source, target, sems.at[number])
        for number, (source, target) in enumerate(
            (
                (rope_hbm, rope_ref),
                (table_hbm, table_ref),
                (lengths_hbm, lengths_ref),
                (head_columns(rot_hbm, block_ref[0], rot_ref.shape[1]), rot_ref),
                (head_columns(query_hbm, block_ref[0], query_ref.shape[1]), query_ref),
                (pages_hbm, key_lat.reshape(pages, page_len, latent)),
            )
        )
    ]
    for copy in copies:
        copy.start()
    copies[0].wait()
    for pair in range(page_len // 2):
        both = rope_ref[:, pair * LANES : (pair + 1) * LANES].astype(jnp.float32)
        keys_rope[pl.ds(2 * pair, pages, stride=page_len), :] = both
        keys_rope[pl.ds(2 * pair + 1, pages, stride=page_len), :] = pltpu.roll(both, ROPE, 1)
    key_rot[...] = keys_rope[...].astype(jnp.bfloat16)
    copies[1].wait()
    copies[2].wait()
    row_ids = lax.broadcasted_iota(jnp.int32, (rows, LANES), 0)
    lengths = jnp.zeros((rows, LANES), jnp.int32)
    for row in range(rows):
        lengths = jnp.where(row_ids == row, lengths_ref[row], lengths)
    lengths = lengths[:, :1]
    key_ids = lax.broadcasted_iota(jnp.int32, (rows, keys), 1)
    page_of, slot_of = key_ids // page_len, key_ids % page_len
    total = jnp.zeros((rows, keys), jnp.float32)
    for step in range(span):
        live = (table_ref[:, step : step + 1] == page_of) & (slot_of + step * page_len < lengths)
        total = total + jnp.where(live, 1.0, 0.0)
    count[...] = total
    copies[3].wait()
    attend_heads(
        query_ref, rot_ref, key_lat, key_rot, count, out_ref, copies[4].wait, copies[5].wait
    )


def attend(block, heads, query_latent, query_rope, cache_latent, cache_rope, page_table, lengths):
    rows = page_table.shape[0]
    pages, page_len, latent = cache_latent.shape
    keys = pages * page_len
    operands = (lengths, page_table, query_latent, query_rope, cache_latent, cache_rope)
    out, *prepared = pl.pallas_call(
        attend_kernel,
        in_specs=[pl.BlockSpec(memory_space=pltpu.SMEM)]
        + [pl.BlockSpec(memory_space=pl.ANY)] * len(operands),
        out_specs=[pl.BlockSpec(memory_space=pltpu.VMEM)] * 4,
        out_shape=[
            pltpu.VMEM((heads * rows, latent), jnp.bfloat16),
            pltpu.VMEM((keys, latent), jnp.bfloat16),
            pltpu.VMEM((keys, LANES), jnp.bfloat16),
            pltpu.VMEM((rows, keys), jnp.float32),
        ],
        scratch_shapes=[
            pltpu.SMEM(lengths.shape, jnp.int32),
            pltpu.VMEM(page_table.shape, jnp.int32),
            pltpu.VMEM((rows, heads * latent), jnp.bfloat16),
            pltpu.VMEM((rows, heads * ROPE), jnp.bfloat16),
            pltpu.VMEM(cache_rope.shape, jnp.bfloat16),
            pltpu.VMEM((keys, LANES), jnp.float32),
            pltpu.SemaphoreType.DMA((len(operands),)),
        ],
        compiler_params=pltpu.CompilerParams(vmem_limit_bytes=16 * MIB),
        cost_estimate=pl.CostEstimate(
            flops=4 * heads * rows * keys * latent,
            bytes_accessed=4 * MIB,
            transcendentals=heads * rows * keys,
        ),
        name="attend",
    )(block.reshape(1).astype(jnp.int32), *[in_hbm(value) for value in operands])
    return out, prepared


def attend_more_kernel(
    staged, block_ref, key_lat, key_rot, count, query_hbm, rot_hbm, *refs
):
    sources, (out_ref, *targets) = refs[:staged], refs[staged : 2 * staged + 1]
    query_ref, rot_ref, sems = refs[2 * staged + 1 :]
    copies = [
        pltpu.make_async_copy(source, target, sems.at[number])
        for number, (source, target) in enumerate(
            (
                (head_columns(rot_hbm, block_ref[0], rot_ref.shape[1]), rot_ref),
                (head_columns(query_hbm, block_ref[0], query_ref.shape[1]), query_ref),
                *zip(sources, targets),
            )
        )
    ]
    for copy in copies:
        copy.start()
    copies[0].wait()
    attend_heads(
        query_ref, rot_ref, key_lat, key_rot, count, out_ref, copies[1].wait, lambda: None
    )
    for copy in copies[2:]:
        copy.wait()


def attend_more(block, heads, prepared, query_latent, query_rope, values):
    key_lat, key_rot, count = prepared
    rows, keys = count.shape
    latent = key_lat.shape[1]
    vmem = pl.BlockSpec(memory_space=pltpu.VMEM)
    anywhere = pl.BlockSpec(memory_space=pl.ANY)
    return pl.pallas_call(
        functools.partial(attend_more_kernel, len(values)),
        in_specs=[pl.BlockSpec(memory_space=pltpu.SMEM)] + [vmem] * 3 + [anywhere] * (2 + len(values)),
        out_specs=[vmem] * (1 + len(values)),
        out_shape=[pltpu.VMEM((heads * rows, latent), jnp.bfloat16)]
        + [pltpu.VMEM(value.shape, value.dtype) for value in values],
        scratch_shapes=[
            pltpu.VMEM((rows, heads * latent), jnp.bfloat16),
            pltpu.VMEM((rows, heads * ROPE), jnp.bfloat16),
            pltpu.SemaphoreType.DMA((2 + len(values),)),
        ],
        compiler_params=pltpu.CompilerParams(vmem_limit_bytes=16 * MIB),
        cost_estimate=pl.CostEstimate(
            flops=4 * heads * rows * keys * latent,
            bytes_accessed=8 * MIB,
            transcendentals=heads * rows * keys,
        ),
        name="attend_more",
    )(
        block.reshape(1).astype(jnp.int32),
        *prepared,
        *[in_hbm(value) for value in (query_latent, query_rope, *values)],
    )


def project_kernel(value_ref, proj_ref, *refs):
    latents, out_ref = refs[:-1], refs[-1]
    heads, latent, width = value_ref.shape
    rows = latents[0].shape[0] // heads
    outs = []
    for head in range(heads):
        both = jnp.concatenate(
            [ref[head * rows : (head + 1) * rows, :] for ref in latents], axis=0
        )
        outs.append(
            jnp.dot(both, value_ref[head], preferred_element_type=jnp.float32).astype(jnp.bfloat16)
        )
    head_out = jnp.concatenate(outs, axis=1)
    chunk = 512
    for begin in range(0, proj_ref.shape[1], chunk):
        out_ref[:, begin : begin + chunk] = jnp.dot(
            head_out, proj_ref[:, begin : begin + chunk], preferred_element_type=jnp.float32
        ).astype(out_ref.dtype)


def project(latents, value_up, out_proj):
    heads, latent, width = value_up.shape
    rows = latents[0].shape[0] // heads
    model = out_proj.shape[1]
    vmem = pl.BlockSpec(memory_space=pltpu.VMEM)
    return pl.pallas_call(
        project_kernel,
        in_specs=[vmem] * (2 + len(latents)),
        out_specs=vmem,
        out_shape=pltpu.VMEM((len(latents) * rows, model), jnp.bfloat16),
        compiler_params=pltpu.CompilerParams(vmem_limit_bytes=16 * MIB),
        cost_estimate=pl.CostEstimate(
            flops=2 * len(latents) * rows * out_proj.size,
            bytes_accessed=2 * (value_up.size + out_proj.size),
            transcendentals=0,
        ),
        name="project",
    )(value_up, out_proj, *latents)


def stage_kernel(count, after_ref, *refs):
    del after_ref
    sources, targets, (token, sems) = refs[:count], refs[count : 2 * count], refs[2 * count :]
    copies = [
        pltpu.make_async_copy(source, target, sems.at[number])
        for number, (source, target) in enumerate(zip(sources, targets))
    ]
    for copy in copies:
        copy.start()
    token[...] = jnp.zeros_like(token)
    for copy in copies:
        copy.wait()


def stage(after, values):
    anywhere = pl.BlockSpec(memory_space=pl.ANY)
    *staged, token = pl.pallas_call(
        functools.partial(stage_kernel, len(values)),
        in_specs=[anywhere] * (1 + len(values)),
        out_specs=[pl.BlockSpec(memory_space=pltpu.VMEM)] * (1 + len(values)),
        out_shape=[pltpu.VMEM(value.shape, value.dtype) for value in values]
        + [jax.ShapeDtypeStruct((8, LANES), jnp.float32)],
        scratch_shapes=[pltpu.SemaphoreType.DMA((len(values),))],
        compiler_params=pltpu.CompilerParams(vmem_limit_bytes=16 * MIB),
        cost_estimate=pl.CostEstimate(
            flops=0,
            bytes_accessed=2 * sum(value.size * value.dtype.itemsize for value in values),
            transcendentals=0,
        ),
        name="stage",
    )(after, *[in_hbm(value) for value in values])
    return staged, token


def lots_of(units):
    return [(begin, min(256, units - begin)) for begin in range(0, units, 256)]


def activate(rows, gate, up):
    gate_values = lax.dot_general(rows, gate, NT, preferred_element_type=jnp.float32)
    up_values = lax.dot_general(rows, up, NT, preferred_element_type=jnp.float32)
    return (gate_values / (1.0 + jnp.exp(-gate_values)) * up_values).astype(jnp.bfloat16)


def expert_kernel(blocks, slot_ref, after_ref, gate_ref, up_ref, down_ref, *refs):
    del after_ref
    inputs, outs, (rows, act) = refs[:blocks], refs[blocks:-2], refs[-2:]
    units, model = gate_ref.shape
    columns = 512
    slot = slot_ref[0]
    tails = min(ref.shape[1] for ref in inputs) - model
    weights, at = [], 0
    for ref in inputs:
        rows[at : at + ref.shape[0], :] = ref[:, :model]
        at += ref.shape[0]
        tail = ref[:, model : model + tails].astype(jnp.float32)
        lane = lax.broadcasted_iota(jnp.int32, tail.shape, 1)
        mine = (lane == slot) | (lane == slot + tail.shape[1] // 2)
        weights.append(jnp.sum(jnp.where(mine, tail, 0.0), axis=1, keepdims=True))
    weight = jnp.concatenate(weights, axis=0)
    for begin, size in lots_of(units):
        lot = pl.ds(begin, size)
        act[:, begin : begin + size] = activate(rows[...], gate_ref[lot, :], up_ref[lot, :])
    for begin in range(0, model, columns):
        terms = weight * jnp.dot(
            act[...], down_ref[:, begin : begin + columns], preferred_element_type=jnp.float32
        )
        at = 0
        for out in outs:
            out[:, begin : begin + columns] = terms[at : at + out.shape[0]].astype(out.dtype)
            at += out.shape[0]


def run_experts(slot, after, gate, up, down, inputs, sizes):
    units, model = gate.shape
    total = sum(block.shape[0] for block in inputs)
    vmem = pl.BlockSpec(memory_space=pltpu.VMEM)
    return pl.pallas_call(
        functools.partial(expert_kernel, len(inputs)),
        in_specs=[pl.BlockSpec(memory_space=pltpu.SMEM), pl.BlockSpec(memory_space=pl.ANY)]
        + [vmem] * (3 + len(inputs)),
        out_specs=[vmem] * len(sizes),
        out_shape=[pltpu.VMEM((size, model), jnp.bfloat16) for size in sizes],
        scratch_shapes=[
            pltpu.VMEM((total, model), jnp.bfloat16),
            pltpu.VMEM((total, units), jnp.bfloat16),
        ],
        compiler_params=pltpu.CompilerParams(vmem_limit_bytes=28 * MIB),
        cost_estimate=pl.CostEstimate(flops=1, bytes_accessed=1, transcendentals=0),
        name="experts",
    )(slot, after, gate, up, down, *inputs)


def all_in_vmem(kernel, name, inputs, shapes):
    vmem = pl.BlockSpec(memory_space=pltpu.VMEM)
    return pl.pallas_call(
        kernel,
        in_specs=[vmem] * len(inputs),
        out_specs=[vmem] * len(shapes),
        out_shape=[pltpu.VMEM(shape, kind) for shape, kind in shapes],
        compiler_params=pltpu.CompilerParams(vmem_limit_bytes=8 * MIB),
        name=name,
    )(*inputs)


def add_kernel(crossed_ref, *refs):
    at = 0
    for mine, out in zip(refs[: len(refs) // 2], refs[len(refs) // 2 :]):
        other = crossed_ref[at : at + mine.shape[0], :]
        total = mine[...].astype(jnp.float32) + other.astype(jnp.float32)
        out[:, : total.shape[1]] = total.astype(out.dtype)
        if out.shape[1] > total.shape[1]:
            out[:, total.shape[1] :] = jnp.zeros((out.shape[0], LANES), out.dtype)
        at += mine.shape[0]


def settle_kernel(mine_ref, crossed_ref, near, line, distant):
    total = mine_ref[...].astype(jnp.float32) + crossed_ref[...].astype(jnp.float32)
    rows = near.shape[0]
    near[...] = total[:rows]
    line[...] = total[rows : 2 * rows].astype(line.dtype)
    distant[...] = total[2 * rows :]


def merge_near_kernel(near_ref, line_ref, pair_ref, away_terms, own_terms, away, mixed):
    own = mixed.shape[0]
    total = near_ref[...] + line_ref[...].astype(jnp.float32)
    away[:, : total.shape[1]] = (total[:own] + away_terms[...]).astype(away.dtype)
    away[:, total.shape[1] :] = jnp.zeros((own, away.shape[1] - total.shape[1]), away.dtype)
    mixed[...] = total[own:] + own_terms[...] + pair_ref[own:, :].astype(jnp.float32)


def merge_far_kernel(distant_ref, *refs):
    arrived, outs = refs[:3], refs[3:]
    total = distant_ref[...]
    for ref in arrived:
        total = total + ref[:, : total.shape[1]].astype(jnp.float32)
    own = outs[0].shape[0]
    for number, out in enumerate(outs):
        piece = total[number * own : (number + 1) * own].astype(out.dtype)
        out[:, : piece.shape[1]] = piece
        if out.shape[1] > piece.shape[1]:
            out[:, piece.shape[1] :] = jnp.zeros((own, out.shape[1] - piece.shape[1]), out.dtype)


def shared_kernel(gate_hbm, up_hbm, down_hbm, after_ref, rows_ref, *refs):
    del after_ref
    outs, (gate, up, down, act, sems) = refs[:-5], refs[-5:]
    rows = outs[0].shape[0]
    units, model = gate.shape
    lots, columns = lots_of(units), 1024
    copies = []
    for number, (begin, size) in enumerate(lots):
        for kind, (source, target) in enumerate(((gate_hbm, gate), (up_hbm, up))):
            lot = pl.ds(begin, size)
            copies.append(
                pltpu.make_async_copy(source.at[lot], target.at[lot], sems.at[kind, number])
            )
    copies.append(pltpu.make_async_copy(down_hbm, down, sems.at[2, 0]))
    for copy in copies:
        copy.start()
    for number, (begin, size) in enumerate(lots):
        copies[2 * number].wait()
        copies[2 * number + 1].wait()
        lot = pl.ds(begin, size)
        act[:, begin : begin + size] = activate(rows_ref[...], gate[lot, :], up[lot, :])
    copies[-1].wait()
    for begin in range(0, model, columns):
        terms = jnp.dot(
            act[...], down[:, begin : begin + columns], preferred_element_type=jnp.float32
        )
        for number, out in enumerate(outs):
            out[:, begin : begin + columns] = terms[number * rows : (number + 1) * rows]


def run_shared(after, rows, parts, gate, up, down):
    units, model = gate.shape
    vmem = pl.BlockSpec(memory_space=pltpu.VMEM)
    anywhere = pl.BlockSpec(memory_space=pl.ANY)
    return pl.pallas_call(
        shared_kernel,
        in_specs=[anywhere] * 4 + [vmem],
        out_specs=[vmem] * parts,
        out_shape=[pltpu.VMEM((rows.shape[0] // parts, model), jnp.float32)] * parts,
        scratch_shapes=[
            pltpu.VMEM(gate.shape, jnp.bfloat16),
            pltpu.VMEM(up.shape, jnp.bfloat16),
            pltpu.VMEM(down.shape, jnp.bfloat16),
            pltpu.VMEM((rows.shape[0], units), jnp.bfloat16),
            pltpu.SemaphoreType.DMA((3, len(lots_of(units)))),
        ],
        compiler_params=pltpu.CompilerParams(vmem_limit_bytes=24 * MIB),
        cost_estimate=pl.CostEstimate(
            flops=6 * rows.shape[0] * units * model,
            bytes_accessed=12 * units * model,
            transcendentals=rows.shape[0] * units,
        ),
        name="shared",
    )(*[in_hbm(value) for value in (gate, up, down)], after, rows)


def exchanges(groups, replicas):
    lines = replicas

    def moves(dz=0, dy=0, dc=0, dx=0):
        pairs = []
        for group in range(groups):
            z, y, core = group // (2 * lines), group // 2 % lines, group % 2
            other = ((z ^ dz) * lines + (y ^ dy)) * 2 + (core ^ dc)
            for rep in range(replicas):
                pairs.append((group * replicas + rep, other * replicas + (rep ^ dx)))
        return pairs

    return lambda value, **by: lax.ppermute(value, AXES, moves(**by))


def route_columns(routes, route_weight, placement):
    experts = placement.shape[0]
    ids = jnp.arange(experts, dtype=jnp.int32)
    slots = jnp.sum(jnp.where(routes[:, :, None] == ids, placement, 0), axis=2)
    table = jnp.sum(jnp.where(slots[:, :, None] == ids, route_weight[:, :, None], 0.0), axis=1)
    half = -(-experts // 64) * 64
    table = jnp.pad(table, ((0, 0), (0, half - experts)))
    high = table.astype(jnp.bfloat16)
    low = (table - high.astype(jnp.float32)).astype(jnp.bfloat16)
    return jnp.concatenate([high, low], axis=1)


def enter(attended, residual):
    attended = attended.astype(jnp.bfloat16).astype(jnp.float32)
    return (residual.astype(jnp.float32) + attended).astype(jnp.bfloat16)


def exchange_experts(swap, pair, columns, slot, weights, shared):
    own, model = pair.shape[0] // 2, pair.shape[1]
    directions = (dict(dx=1), dict(dy=1), dict(dx=1, dy=1))
    rows = jnp.concatenate([pair, columns], axis=1)
    line = [swap(rows[own:], dz=step) for step in (3, 2, 1)][::-1]
    across = swap(rows, dy=1)
    distant = jnp.concatenate(line, axis=0)
    wide = jnp.concatenate([distant, jnp.zeros((distant.shape[0], LANES), distant.dtype)], axis=1)
    distant, wide, slot = lax.optimization_barrier((distant, wide, slot))
    sent = (distant, distant, wide)
    planes = [swap(value, **by) for value, by in zip(sent, directions)]
    early = [rows, across, distant]
    depth, width = sum(value.shape[0] for value in early), distant.shape[0]
    weights, token = stage(distant, weights)
    early += [swap(value, dc=1) for value in early]
    first = list(run_experts(slot, token, *weights, early, [depth, depth]))
    *planes, first[0], first[1] = lax.optimization_barrier((*planes, first[0], first[1]))
    others = [swap(plane, dc=1) for plane in planes]
    last = run_experts(slot, token, *weights, [*planes, *others], [width] * 3 + [3 * width])
    near, back, distant_sum = all_in_vmem(
        settle_kernel,
        "settle",
        [first[0], swap(first[1], dc=1)],
        [
            ((2 * own, model), jnp.float32),
            ((2 * own, model), jnp.bfloat16),
            ((width, model), jnp.float32),
        ],
    )
    crossed, back = last[3], swap(back, dy=1)
    sums = all_in_vmem(
        add_kernel,
        "add",
        [swap(crossed, dc=1), *last[:3]],
        [((width, model + more), jnp.bfloat16) for more in (0, LANES, 0)],
    )
    returned = [swap(value, **by) for value, by in zip(sums, directions)]
    away_terms, own_terms = run_shared(sums[0], pair, 2, *shared)
    *returned, away_terms, own_terms = lax.optimization_barrier(
        (*returned, away_terms, own_terms)
    )
    away, mixed = all_in_vmem(
        merge_near_kernel,
        "merge_near",
        [near, back, pair, away_terms, own_terms],
        [((own, model + LANES), jnp.bfloat16), ((own, model), jnp.float32)],
    )
    pieces = all_in_vmem(
        merge_far_kernel,
        "merge_far",
        [distant_sum, *returned],
        [((own, model + more), jnp.bfloat16) for more in (0, 2 * LANES, 2 * LANES)],
    )
    pieces = [swap(piece, dz=step) for step, piece in zip((1, 2, 3), pieces)]
    return mixed, [*pieces, swap(away, dx=1)]


def finish_kernel(mixed_ref, gain_ref, *refs):
    pieces, out = refs[:-1], refs[-1]
    mixed = mixed_ref[...]
    for piece in pieces:
        mixed = mixed + piece[:, : mixed.shape[1]].astype(jnp.float32)
    inverse = lax.rsqrt(jnp.mean(mixed * mixed, axis=1, keepdims=True) + EPSILON)
    out[...] = (mixed * inverse * gain_ref[...]).astype(out.dtype)


def finish(mixed, norm_gain, pieces=()):
    vmem = pl.BlockSpec(memory_space=pltpu.VMEM)
    return pl.pallas_call(
        finish_kernel,
        in_specs=[vmem] * (2 + len(pieces)),
        out_specs=vmem,
        out_shape=jax.ShapeDtypeStruct(mixed.shape, jnp.bfloat16),
        compiler_params=pltpu.CompilerParams(vmem_limit_bytes=8 * MIB),
        name="finish",
    )(mixed, norm_gain.reshape(1, -1), *pieces)


def per_device(
    residual,
    query_latent,
    query_rope,
    cache_latent,
    cache_rope,
    page_table,
    lengths,
    value_up,
    out_proj,
    routes,
    route_weight,
    placement,
    expert_gate,
    expert_up,
    expert_down,
    shared_gate,
    shared_up,
    shared_down,
    norm_gain,
):
    replicas = lax.axis_size("rep")
    groups = lax.axis_size("ep")
    rep = lax.axis_index("rep")
    slot = lax.axis_index("ep").reshape(1).astype(jnp.int32)
    own = page_table.shape[0]
    heads = value_up.shape[0]
    own_rows = lambda value: lax.dynamic_slice_in_dim(value, rep * own, own, 0)
    caches = (query_latent, query_rope, cache_latent, cache_rope, page_table, lengths)
    gate = expert_gate[0].T
    up = expert_up[0].T
    down = expert_down[0]
    shared = (shared_gate.T, shared_up.T, shared_down)
    if replicas == 2 and groups == 16:
        swap = exchanges(groups, replicas)
        own_last = lambda value: lax.dynamic_slice_in_dim(
            jnp.concatenate([value, value], axis=0), (1 - rep) * own, 2 * own, 0
        )
        away, prepared = attend(1 - rep, heads, *caches)
        arrived = swap(away, dx=1)
        kept, value_up, out_proj = attend_more(
            rep, heads, prepared, query_latent, query_rope, (value_up, out_proj)
        )
        terms = project([arrived, kept], value_up, out_proj)
        terms, routing = lax.optimization_barrier((terms, (routes, route_weight, residual)))
        routes, route_weight, residual = routing
        back = swap(terms, dx=1)
        columns = own_last(route_columns(routes, route_weight, placement))
        residual = own_last(residual)
        back = jnp.concatenate([back[own:], back[:own]], axis=0)
        pair = enter(terms.astype(jnp.float32) + back.astype(jnp.float32), residual)
        mixed, pieces = exchange_experts(swap, pair, columns, slot, (gate, up, down), shared)
        return finish(mixed, norm_gain, pieces)

    latents, _ = attend(jnp.int32(0), heads * replicas, *caches)
    latents = lax.all_to_all(latents, "rep", 0, 0, tiled=True)
    latents = latents.reshape(replicas, -1, latents.shape[1])
    terms = project([latents[i] for i in range(replicas)], value_up, out_proj)
    attended = lax.psum_scatter(terms, "rep", scatter_dimension=0, tiled=True)
    hidden = enter(attended, own_rows(residual))
    model = hidden.shape[1]
    columns = route_columns(own_rows(routes), own_rows(route_weight), placement)
    block = jnp.concatenate([hidden, columns], axis=1)
    every = lax.all_gather(block, AXES, axis=0, tiled=True)
    lot = min(512, every.shape[0])
    terms = [
        run_experts(slot, slot, gate, up, down, [every[at : at + lot]], [lot])[0]
        for at in range(0, every.shape[0], lot)
    ]
    mine = lax.dynamic_slice_in_dim(every, slot[0] * replicas * own, replicas * own, 0)[:, :model]
    own_terms = run_shared(mine, mine, 1, *shared)[0].astype(jnp.bfloat16)
    total = lax.psum_scatter(
        jnp.concatenate(terms, axis=0), AXES, scatter_dimension=0, tiled=True
    ).astype(jnp.float32)
    total = total + lax.psum_scatter(
        own_terms, "rep", scatter_dimension=0, tiled=True
    ).astype(jnp.float32)
    return finish(hidden.astype(jnp.float32) + total, norm_gain)


def solution(mesh):
    in_specs = (
        P("ep", None),
        P(("ep", "rep"), None),
        P(("ep", "rep"), None),
        P(("ep", "rep"), None, None),
        P(("ep", "rep"), None),
        P(("ep", "rep"), None),
        P(("ep", "rep")),
        P("rep", None, None),
        P("rep", None),
        P("ep", None),
        P("ep", None),
        P(),
        P("ep", None, "rep"),
        P("ep", None, "rep"),
        P("ep", "rep", None),
        P(None, "rep"),
        P(None, "rep"),
        P("rep", None),
        P(),
    )
    out_specs = P(("ep", "rep"), None)
    return jax.shard_map(
        per_device, mesh=mesh, in_specs=in_specs, out_specs=out_specs, check_vma=False
    )
```
